32 devices in a mesh: dp: 2 (over core), expert: 16 (over z, y, x).
Axes of the slice: x: 2, y: 2, z: 4, core: 2. Of those that a mesh axis runs over, the one named last changes fastest.
Arguments:
- tokens: bfloat16 [2048, 3584], P('expert', 'dp'), may hold values from -6 to 6
- out_grad: bfloat16 [2048, 3584], P('expert', 'dp'), may hold values from -6 to 6
- gate_up_weight: bfloat16 [16, 3584, 2048], P('expert', 'dp'), may hold values from -0.09375 to 0.09375
- down_weight: bfloat16 [16, 1024, 3584], P('expert', None, 'dp'), may hold values from -0.1875 to 0.1875
- routes: int32 [2048, 2], P('expert'), may hold values from 0 to 15, all different within a row; in each aligned block of 128 rows (0 to 127, 128 to 255, ...) at most 32 rows name the same one
- route_weight: float32 [2048, 2], P('expert'), may hold values from 0.1 to 1
- swapped: int32 [4], replicated, may hold values from 0 to 7, as said below
Outputs:
- layer_out: bfloat16 [2048, 3584], P('expert', 'dp')
- token_grad: bfloat16 [2048, 3584], P('expert', 'dp')
- down_grad: bfloat16 [16, 1024, 3584], P('expert', None, 'dp')
The draws below stay inside these ranges and needn't reach their ends.
Inputs may be any that keep to these rules, and one draw needn't show every extreme that they name: `routes`: among the rows of each block of 128 consecutive tokens, no expert is named more than 32 times, a bound that some block reaches; a token names different experts. `swapped`: 4 different device numbers; device 0 and device 8 - 1 are always among them.
All inputs are finite; a program needn't handle non-finite values.
Results may differ from the reference program's by a relative error of at most 0.023.
Values may be sent and summed in bfloat16 or wider, within the bound.
No kernel may reach another device: no remote copies, remote signals or barrier semaphores. Data moves between devices by JAX's collectives and lax.ppermute only.
A program may use at most 64 MiB of HBM per device.

```python
import math
import jax
import jax.numpy as jnp
import numpy as np
from jax import lax

D = 3584
FF = 1024
TOP = 2
MIGR = 4
TOK_DEV = 128
EXPERTS = 16
PAIRS_ALL = 8
CAP = 32
TOKENS = 2048
N_DP = 2


def draw_swapped(key, part):
    inner = 1 + jax.random.permutation(jax.random.fold_in(key, 11), PAIRS_ALL - 2)[:MIGR - 2]
    listed = jnp.concatenate([jnp.zeros((1,), jnp.int32), inner.astype(jnp.int32), jnp.full((1,), PAIRS_ALL - 1, jnp.int32)])
    order = jax.random.permutation(jax.random.fold_in(key, 12), MIGR)
    return listed[order].astype(jnp.int32)


def steps_of(key, extent, shards, least, high):
    factor_of = 1.0
    for axis_at, blocks in shards:
        steps = jax.random.uniform(jax.random.fold_in(jax.random.fold_in(key, 6), axis_at), (blocks,), jnp.float32, least / len(shards), high / len(shards))
        factor_of = factor_of * jnp.repeat(jnp.exp(steps), extent[axis_at] // blocks).reshape((-1,) + (1,) * (len(extent) - 1 - axis_at))
    return factor_of


def deal_out(key, own, number, rows, count, top, reach, lean):
    ranking = jax.random.permutation(key, count)
    crowded, usual = portions_of(count, rows * top, reach, lean, True), portions_of(count, rows * top, reach, lean, False)
    places = jnp.arange(count)

    def named(tallies, turn):
        used = int((tallies > 0).sum())
        fixed = max(1, used // 4)
        passed = fixed + (places - fixed + turn * (used - fixed)) % max(1, count - fixed)
        return jnp.zeros((count,), jnp.int32).at[ranking[jnp.where(places < fixed, places, passed)]].set(jnp.asarray(tallies, jnp.int32))

    tallies = jnp.where(number % 4 == 0, named(crowded, number // 4), named(usual, number - number // 4 - 1))
    mixed = jax.random.permutation(jax.random.fold_in(own, 3), count)
    source_of, receiver = mixed[0:count // 2 * 2:2], mixed[1:count // 2 * 2:2]
    slack = jnp.minimum(tallies[source_of] - 1, reach - tallies[receiver]) // 2
    slack = jnp.where((source_of == ranking[0]) | (receiver == ranking[0]) | (tallies[receiver] == 0), 0, jnp.maximum(slack, 0))
    passed = jax.random.randint(jax.random.fold_in(own, 4), (count // 2,), 0, 1 << 20) % (slack + 1)
    tallies = tallies.at[source_of].add(-passed).at[receiver].add(passed)
    members = jnp.searchsorted(jnp.cumsum(tallies), jnp.arange(rows * top), side="right").astype(jnp.int32)
    listing = members.reshape(top, rows).T
    listing = listing[jax.random.permutation(jax.random.fold_in(own, 1), rows)]
    turn = jax.random.randint(jax.random.fold_in(own, 2), (rows, 1), 0, top)
    return jnp.take_along_axis(listing, (jnp.arange(top)[None, :] + turn) % top, axis=1)


def portions_of(count, total, limit, lean, full):
    portions = [(1 << 20) // math.isqrt(rank ** lean) + 1 for rank in range(1, count + 1)]
    largest = limit if full else min(limit, max(-(-total // count), total * portions[0] // sum(portions)))
    least = 1 if total - largest >= count - 1 else 0
    counts, rest = [largest] + [least] * (count - 1), total - largest - least * (count - 1)
    while rest > 0:
        movable = [i for i in range(1, count) if counts[i] < largest] or [i for i in range(1, count) if counts[i] < limit]
        whole, remaining = sum([portions[i] for i in movable]), rest
        for i in movable:
            extra = min(limit - counts[i], max(1, remaining * portions[i] // whole), rest)
            counts[i] = counts[i] + extra
            rest = rest - extra
    return np.array(counts)


def bell_draw(key, shape, width, most, split=(), kind=jnp.bfloat16):
    level = steps_of(key, shape, split, -0.22, 0.18) if split else 1.0
    result = jax.random.normal(key, shape, jnp.float32) * width * level
    return jnp.minimum(jnp.maximum(result, -most), most).astype(kind)


def setup_inputs(seed: int = 0) -> dict:
    splits = jax.random.split(jax.random.key(seed), 8)
    tokens = bell_draw(splits[0], (TOKENS, D), 1.0, 6.0, ((0, 16), (1, 2)))
    out_grad = bell_draw(splits[1], (TOKENS, D), 1.0, 6.0, ((0, 16), (1, 2)))
    gate_up_weight = bell_draw(splits[2], (EXPERTS, D, 2 * FF), D ** -0.5, 0.09375, ((0, 16), (1, 2)))
    down_weight = bell_draw(splits[3], (EXPERTS, FF, D), FF ** -0.5, 0.1875, ((0, 16), (2, 2)))
    routes_keys = jax.random.split(jax.random.fold_in(splits[4], 1), TOKENS // TOK_DEV)
    routes_turns = jax.random.permutation(jax.random.fold_in(splits[4], 3), TOKENS // TOK_DEV)
    routes = jax.vmap(lambda own, number: deal_out(jax.random.fold_in(splits[4], 2), own, number, TOK_DEV, EXPERTS, TOP, CAP, 2))(routes_keys, routes_turns).reshape((TOKENS, TOP))
    route_weight = jnp.clip(jnp.exp(math.log(1.0) - 2.3025851 * jax.random.uniform(splits[5], (TOKENS, TOP), jnp.float32) ** steps_of(splits[5], (TOKENS, TOP), ((0, 16),), -0.2, 0.2)), 0.1, 1.0)
    swapped = draw_swapped(jax.random.fold_in(splits[7], 71), 0)
    return {"tokens": tokens, "out_grad": out_grad, "gate_up_weight": gate_up_weight, "down_weight": down_weight, "routes": routes, "route_weight": route_weight, "swapped": swapped}


def block_sum(left, right, pattern):
    parts = jnp.einsum(pattern, left, right)
    rounded = lax.optimization_barrier(parts.astype(jnp.bfloat16))
    return jnp.sum(rounded.astype(jnp.float32), axis=0)


def reference(tokens, out_grad, gate_up_weight, down_weight, routes, route_weight, swapped):
    total_rows = TOKENS * TOP
    block_rows = TOK_DEV * TOP
    buffer_rows = (TOKENS // TOK_DEV) * CAP
    width_block = D // N_DP
    flat = routes.reshape(-1).astype(jnp.int32)
    column = (jnp.arange(total_rows, dtype=jnp.int32) // block_rows).astype(jnp.int32)
    onehot = (flat[:, None] == jnp.arange(EXPERTS, dtype=jnp.int32)[None, :]).astype(jnp.int32)
    running = jnp.cumsum(onehot.reshape(TOKENS // TOK_DEV, block_rows, EXPERTS), axis=1).reshape(total_rows, EXPERTS)
    slot = jnp.sum(running * onehot, axis=1).astype(jnp.int32) - 1
    spot = flat * buffer_rows + column * CAP + slot
    table = jnp.full((EXPERTS * buffer_rows,), total_rows, jnp.int32)
    table = table.at[spot].set(jnp.arange(total_rows, dtype=jnp.int32)).reshape(EXPERTS, buffer_rows)
    token_pad = jnp.concatenate([tokens, jnp.zeros((1, D), jnp.bfloat16)], axis=0)
    grad_pad = jnp.concatenate([out_grad, jnp.zeros((1, D), jnp.bfloat16)], axis=0)
    weight_pad = jnp.concatenate([route_weight.reshape(-1), jnp.zeros((1,), jnp.float32)], axis=0)

    def per_expert(carry, inputs):
        out_acc, dx_acc = carry
        rows, w_gate_up, w_down = inputs
        token_index = rows // TOP
        weights = weight_pad[rows]
        token_rows = token_pad[token_index]
        row_grad = (weights[:, None] * grad_pad[token_index].astype(jnp.float32)).astype(jnp.bfloat16)
        left = token_rows.astype(jnp.float32).reshape(buffer_rows, N_DP, width_block)
        right = w_gate_up.astype(jnp.float32).reshape(N_DP, width_block, 2 * FF)
        gate_up = block_sum(left, right, "rbk,bkf->brf")
        gate_val = gate_up[:, :FF]
        up_val = gate_up[:, FF:]
        sig = jax.nn.sigmoid(gate_val)
        act = gate_val * sig
        hidden = (act * up_val).astype(jnp.bfloat16)
        row_out = jnp.dot(hidden, w_down, preferred_element_type=jnp.float32).astype(jnp.bfloat16)
        grad_left = row_grad.astype(jnp.float32).reshape(buffer_rows, N_DP, width_block)
        down_right = w_down.astype(jnp.float32).reshape(FF, N_DP, width_block)
        hidden_grad = block_sum(grad_left, down_right, "rbk,fbk->brf")
        gate_grad = hidden_grad * up_val * sig * (1.0 + gate_val * (1.0 - sig))
        up_grad = hidden_grad * act
        gate_up_grad = jnp.concatenate([gate_grad, up_grad], axis=1).astype(jnp.bfloat16)
        row_dx = lax.dot_general(gate_up_grad, w_gate_up, (((1,), (1,)), ((), ())), preferred_element_type=jnp.float32).astype(jnp.bfloat16)
        expert_grad = lax.dot_general(hidden, row_grad, (((0,), (0,)), ((), ())), preferred_element_type=jnp.float32).astype(jnp.bfloat16)
        out_acc = out_acc.at[token_index].add(weights[:, None] * row_out.astype(jnp.float32))
        dx_acc = dx_acc.at[token_index].add(row_dx.astype(jnp.float32))
        return (out_acc, dx_acc), expert_grad

    start = (jnp.zeros((TOKENS + 1, D), jnp.float32), jnp.zeros((TOKENS + 1, D), jnp.float32))
    (out_acc, dx_acc), expert_grad = lax.scan(per_expert, start, (table, gate_up_weight, down_weight))
    layer_out = out_acc[:TOKENS].astype(jnp.bfloat16)
    token_grad = dx_acc[:TOKENS].astype(jnp.bfloat16)
    moved = jnp.any(swapped[:, None] == jnp.arange(PAIRS_ALL, dtype=jnp.int32)[None, :], axis=0)
    device_ids = jnp.arange(EXPERTS, dtype=jnp.int32)
    host = jnp.where(moved[device_ids % PAIRS_ALL], (device_ids + PAIRS_ALL) % EXPERTS, device_ids).astype(jnp.int32)
    down_grad = expert_grad[host]
    return layer_out, token_grad, down_grad
```

```python
import jax
import jax.numpy as jnp
from jax import lax
from jax.sharding import PartitionSpec as P

BF16 = jnp.bfloat16
F32 = jnp.float32


def crossed(block, axis, distance):
    size = lax.axis_size(axis)
    return lax.ppermute(block, axis, [(i, (i + distance) % size) for i in range(size)])


def summed_blocks(part):
    total = part.astype(F32)
    for distance in range(1, lax.axis_size("dp")):
        total = total + crossed(part, "dp", distance).astype(F32)
    return total


def halves_exchange(rows, half):
    groups = [[side * half + j for j in range(half)] for side in range(2)]
    return lax.all_to_all(
        rows, "expert", split_axis=0, concat_axis=0, tiled=True, axis_index_groups=groups
    )


def slots_of(routes, experts):
    ids = jnp.arange(experts, dtype=jnp.int32)
    member = jnp.any(routes[:, :, None] == ids, axis=1)
    count = routes.shape[0]
    before = jnp.arange(count)[:, None] > jnp.arange(count)[None, :]
    place = jnp.dot(before.astype(BF16), member.astype(BF16), preferred_element_type=F32)
    return jnp.where(member, place.astype(jnp.int32), -1)


def chooser(places, first, half, capacity):
    mine = lax.dynamic_slice_in_dim(places, first, half, axis=1)
    return (mine.T[:, None, :] == jnp.arange(capacity)[None, :, None]).astype(F32)


def on_device(tokens, out_grad, gate_up_weight, down_weight, routes, route_weight, swapped):
    experts = lax.axis_size("expert")
    half = experts // 2
    token_count, width = tokens.shape
    top_count = routes.shape[1]
    hidden_width = down_weight.shape[1]
    capacity = max(2, 2 * token_count * top_count // experts)
    n_dp = lax.axis_size("dp")
    me = lax.axis_index("expert")
    side = me // half
    moved = jnp.any(swapped == me % half)

    meta = jnp.concatenate([routes.astype(F32), route_weight], axis=1)
    meta_far = crossed(meta, "expert", half)
    tokens_far = crossed(tokens, "expert", half)
    grad_far = crossed(out_grad, "expert", half)
    routes_far = meta_far[:, :top_count].astype(jnp.int32)
    weight_far = meta_far[:, top_count:]

    places = slots_of(routes, experts)
    places_far = slots_of(routes_far, experts)
    rows = 2 * half * capacity

    def selector(first, swap):
        near = chooser(places, first, half, capacity)
        far = chooser(places_far, first, half, capacity)
        zero = jnp.zeros_like(near)
        both = [jnp.concatenate([near, zero], axis=2), jnp.concatenate([zero, far], axis=2)]
        if swap:
            both = both[::-1]
        return jnp.concatenate(both, axis=1).reshape(rows, 2 * token_count)

    def weights_at(first):
        ids = first + jnp.arange(half, dtype=jnp.int32)

        def table(r, w):
            return jnp.sum(jnp.where(r[:, :, None] == ids, w[:, :, None], 0.0), axis=1)

        return jnp.concatenate([table(routes, route_weight), table(routes_far, weight_far)], axis=0)

    def weighted(sel, first):
        w = weights_at(first).T[:, None, :]
        return (sel.reshape(half, 2 * capacity, 2 * token_count) * w).reshape(sel.shape)

    here = side * half
    there = half - here
    sel = selector(here, False)
    sel_w = weighted(sel, here)
    row_w = jnp.sum(sel_w, axis=1, keepdims=True)
    sel_there = selector(there, True)
    row_w_there = jnp.sum(weighted(sel_there, there), axis=1, keepdims=True)
    sel16 = sel.astype(BF16)

    def pick(s, data):
        return jnp.dot(s.astype(BF16), data, preferred_element_type=F32)

    def exchange(x):
        return halves_exchange(x.reshape(half, 2 * capacity, width), half).reshape(rows, width)

    tokens_both = jnp.concatenate([tokens, tokens_far], axis=0)
    grad_both = jnp.concatenate([out_grad, grad_far], axis=0)
    recv_tokens = exchange(pick(sel16, tokens_both).astype(BF16))
    recv_grads = exchange((pick(sel16, grad_both) * row_w).astype(BF16))

    local_gate_up = gate_up_weight[0]
    local_down = down_weight[0]
    gate_up_part = jnp.dot(recv_tokens, local_gate_up, preferred_element_type=F32).astype(BF16)
    gate_up = summed_blocks(gate_up_part)
    gate_val = gate_up[:, :hidden_width]
    up_val = gate_up[:, hidden_width:]
    sig = jax.nn.sigmoid(gate_val)
    act = gate_val * sig
    hidden = (act * up_val).astype(BF16)
    row_out = jnp.dot(hidden, local_down, preferred_element_type=F32).astype(BF16)
    back_out = exchange(row_out)

    hidden_part = lax.dot_general(
        recv_grads, local_down, (((1,), (1,)), ((), ())), preferred_element_type=F32
    ).astype(BF16)
    hidden_grad = summed_blocks(hidden_part)
    gate_grad = hidden_grad * up_val * sig * (1.0 + gate_val * (1.0 - sig))
    up_grad = hidden_grad * act
    gate_up_grad = jnp.concatenate([gate_grad, up_grad], axis=1).astype(BF16)
    row_dx = lax.dot_general(
        gate_up_grad, local_gate_up, (((1,), (1,)), ((), ())), preferred_element_type=F32
    ).astype(BF16)
    back_dx = exchange(row_dx)

    share = hidden_width // n_dp
    core = lax.axis_index("dp")
    mine = lax.dynamic_slice_in_dim(hidden, core * share, share, axis=1)
    far_share = crossed(mine, "expert", half)
    far_hidden = jnp.zeros_like(hidden)
    for distance in range(n_dp):
        piece = far_share if distance == 0 else crossed(far_share, "dp", distance)
        far_hidden = lax.dynamic_update_slice_in_dim(
            far_hidden, piece, ((core - distance) % n_dp) * share, axis=1
        )
    grads_there = exchange((pick(sel_there, grad_both) * row_w_there).astype(BF16))
    left = jnp.where(moved, far_hidden, hidden)
    right = jnp.where(moved, grads_there, recv_grads)
    down_grad = lax.dot_general(
        left, right, (((0,), (0,)), ((), ())), preferred_element_type=F32
    ).astype(BF16)[None]

    def give(s, data):
        return lax.dot_general(s, data, (((0,), (0,)), ((), ())), preferred_element_type=F32)

    w_hi = sel_w.astype(BF16)
    w_lo = (sel_w - w_hi.astype(F32)).astype(BF16)
    part_out = give(w_hi, back_out) + give(w_lo, back_out)
    part_dx = give(sel16, back_dx)

    def finish(part):
        far = crossed(part[token_count:].astype(BF16), "expert", half)
        return (part[:token_count] + far.astype(F32)).astype(BF16)

    return finish(part_out), finish(part_dx), down_grad


def solution(mesh):
    return jax.shard_map(
        on_device,
        mesh=mesh,
        in_specs=(
            P("expert", "dp"),
            P("expert", "dp"),
            P("expert", "dp", None),
            P("expert", None, "dp"),
            P("expert", None),
            P("expert", None),
            P(),
        ),
        out_specs=(P("expert", "dp"), P("expert", "dp"), P("expert", None, "dp")),
        check_vma=False,
    )
```

```python
import jax
import jax.numpy as jnp
from jax import lax
from jax.experimental import pallas as pl
from jax.experimental.pallas import tpu as pltpu
from jax.sharding import PartitionSpec as P

BF16 = jnp.bfloat16
F32 = jnp.float32
LONG = 50_000_000_000
ANYWHERE = pl.BlockSpec(memory_space=pl.ANY)
IN_VMEM = pl.BlockSpec(memory_space=pltpu.VMEM)


def tile_of(size):
    return 256 if size % 256 == 0 else size


def wide_tile_of(size):
    return size // 2 if size % 256 == 0 else size


def run(body, out_shape, grid, in_specs, out_specs, operands, scratch=(), deps=(), aliases=None, flops=0):
    count = len(operands)
    out_shape = jax.tree.map(
        lambda x: pltpu.HBM(x.shape, x.dtype) if isinstance(x, jax.ShapeDtypeStruct) else x,
        out_shape,
        is_leaf=lambda x: not isinstance(x, (list, tuple)),
    )

    def whole(*refs):
        body(*refs[:count], *refs[count + len(deps) :])

    return pl.pallas_call(
        whole,
        out_shape=out_shape,
        grid=grid,
        in_specs=list(in_specs) + [ANYWHERE] * len(deps),
        out_specs=out_specs,
        scratch_shapes=list(scratch),
        input_output_aliases=aliases or {},
        cost_estimate=pl.CostEstimate(flops=flops, bytes_accessed=0, transcendentals=0),
        compiler_params=pltpu.CompilerParams(vmem_limit_bytes=52 * 1024 * 1024),
    )(*operands, *deps)


def tied(value, *deps, flops=0):
    shape = jax.ShapeDtypeStruct(value.shape, value.dtype)
    return run(lambda *refs: None, shape, (), [ANYWHERE], ANYWHERE, [value], (), deps, {0: 0}, flops)


def resident(weight):
    parts = 8
    step = weight.shape[1] // parts

    def body(w_ref, out, sems):
        copies = [
            pltpu.make_async_copy(
                w_ref.at[0, pl.ds(n * step, step)], out.at[0, pl.ds(n * step, step)], sems.at[n]
            )
            for n in range(parts)
        ]
        for copy in copies:
            copy.start()
        for copy in copies:
            copy.wait()

    return run(
        body,
        pltpu.VMEM(weight.shape, weight.dtype),
        (),
        [ANYWHERE],
        IN_VMEM,
        [weight],
        [pltpu.SemaphoreType.DMA((parts,))],
    )


def held(value, *deps):
    def body(value_ref, out, sem):
        copy = pltpu.make_async_copy(value_ref, out, sem)
        copy.start()
        copy.wait()

    shape = jax.ShapeDtypeStruct(value.shape, value.dtype)
    scratch = [pltpu.SemaphoreType.DMA]
    return run(body, shape, (), [ANYWHERE], ANYWHERE, [value], scratch, deps)


def fixed(shape):
    return pl.BlockSpec(shape, lambda *at: (0,) * len(shape))


def pick(parts, peers, deps=(), flops=0):
    rows = parts[0][0].shape[0]
    slots = rows // peers
    count, width = parts[0][1].shape
    tile = wide_tile_of(width)
    operands, specs = [], []
    for sel, data, weight in parts:
        operands += [sel, data]
        specs += [fixed(sel.shape), pl.BlockSpec((count, tile), lambda c: (0, c))]
        if weight is not None:
            operands.append(weight)
            specs.append(fixed(weight.shape))

    def body(*refs):
        out, refs = refs[-1], list(refs[:-1])
        for n, (_, _, weight) in enumerate(parts):
            got = jnp.dot(refs.pop(0)[...], refs.pop(0)[...], preferred_element_type=F32)
            if weight is not None:
                got = got * refs.pop(0)[...]
            out[:, n * slots : (n + 1) * slots, :] = got.astype(BF16).reshape(peers, slots, tile)

    return run(
        body,
        jax.ShapeDtypeStruct((peers, slots * len(parts), width), BF16),
        (width // tile,),
        specs,
        pl.BlockSpec((peers, slots * len(parts), tile), lambda c: (0, 0, c)),
        operands,
        deps=deps,
        flops=flops,
    )


def tile_at(tile, size):
    if tile == size:
        return slice(None)
    return pl.ds(pl.multiple_of(pl.program_id(0) * tile, tile), tile)


def gate_up_part(x, group, slots, weight, deps=()):
    peers, _, width = x.shape
    rows, columns = peers * slots, weight.shape[2]
    tile = tile_of(columns // 2) * 2

    def body(x_ref, w_ref, out):
        got = jnp.dot(x_ref[...].reshape(rows, width), w_ref[0, :, tile_at(tile, columns)], preferred_element_type=F32)
        out[...] = got.astype(BF16)

    return run(
        body,
        jax.ShapeDtypeStruct((rows, columns), BF16),
        (columns // tile,),
        [
            pl.BlockSpec((peers, slots, width), lambda c: (0, group, 0)),
            IN_VMEM,
        ],
        pl.BlockSpec((rows, tile), lambda c: (0, c)),
        [x, weight],
        deps=deps,
    )


def total(refs):
    result = refs[0][...].astype(F32)
    for ref in refs[1:]:
        result = result + ref[...].astype(F32)
    return result


def hidden_and_out(near, far, weight, core, n_dp, peers, tail, deps=()):
    n = len(near)
    rows = near[0].shape[0]
    _, inner, width = weight.shape
    slots = rows // peers
    share = inner // n_dp
    tile = wide_tile_of(width)
    block = pl.BlockSpec((peers, slots, tile), lambda c: (0, 0, c))

    def body(*refs):
        near_refs, far_refs = refs[:n], refs[n : 2 * n]
        core_ref, w_ref, tail_ref, hidden, mine, send, out = refs[2 * n :]

        @pl.when(pl.program_id(0) == 0)
        def _():
            for at, part_refs in ((0, near_refs), (rows, far_refs)):
                gate_up = total(part_refs)
                gate = gate_up[:, :inner]
                hidden[at : at + rows, :] = (
                    gate * jax.nn.sigmoid(gate) * gate_up[:, inner:]
                ).astype(BF16)
            first = pl.multiple_of(core_ref[0] * share, 128)
            mine[...] = hidden[:, pl.ds(first, share)]

        got = jnp.dot(
            hidden[...], w_ref[0, :, tile_at(tile, width)], preferred_element_type=F32
        ).astype(BF16)
        out[...] = got[:rows].reshape(peers, slots, tile)
        send[:, :slots, :] = got[rows:].reshape(peers, slots, tile)
        send[:, slots:, :] = tail_ref[...]

    return run(
        body,
        (
            jax.ShapeDtypeStruct((2 * rows, inner), BF16),
            jax.ShapeDtypeStruct((2 * rows, share), BF16),
            jax.ShapeDtypeStruct((peers, 2 * slots, width), BF16),
            jax.ShapeDtypeStruct((peers, slots, width), BF16),
        ),
        (width // tile,),
        [fixed(p.shape) for p in (*near, *far)]
        + [pl.BlockSpec(memory_space=pltpu.SMEM), IN_VMEM, block],
        (
            fixed((2 * rows, inner)),
            fixed((2 * rows, share)),
            pl.BlockSpec((peers, 2 * slots, tile), lambda c: (0, 0, c)),
            block,
        ),
        [*near, *far, core, weight, tail],
        deps=deps,
    )


def hidden_grad_part(x, slots, weight, deps=()):
    peers, _, width = x.shape
    rows, inner = peers * slots, weight.shape[1]
    tile = tile_of(inner)

    def body(x_ref, w_ref, out):
        data = [x_ref[:, at : at + slots, :].reshape(rows, width) for at in (0, slots)]
        got = lax.dot_general(
            jnp.concatenate(data, axis=0),
            w_ref[0, tile_at(tile, inner), :],
            (((1,), (1,)), ((), ())),
            preferred_element_type=F32,
        )
        out[...] = got.astype(BF16)

    return run(
        body,
        jax.ShapeDtypeStruct((2 * rows, inner), BF16),
        (inner // tile,),
        [fixed(x.shape), IN_VMEM],
        pl.BlockSpec((2 * rows, tile), lambda c: (0, c)),
        [x, weight],
        deps=deps,
    )


def rows_dx(grad_parts, near, far, weight, peers, ahead, tail, deps=()):
    n = len(near)
    rows = near[0].shape[0]
    inner = grad_parts[0].shape[1]
    width = weight.shape[1]
    slots = rows // peers
    tile = tile_of(width)
    block = pl.BlockSpec((peers, slots, tile), lambda c: (0, 0, c))
    blocks = pl.BlockSpec((peers, 2 * slots, tile), lambda c: (0, 0, c))

    def body(*refs):
        grad_refs, near_refs, far_refs = refs[:n], refs[n : 2 * n], refs[2 * n : 3 * n]
        w_ref, ahead_ref, tail_ref, far_out, near_out, both = refs[3 * n :]

        @pl.when(pl.program_id(0) == 0)
        def _():
            for at, part_refs in ((0, near_refs), (rows, far_refs)):
                hidden_grad = total([g.at[at : at + rows, :] for g in grad_refs])
                gate_up = total(part_refs)
                gate, up = gate_up[:, :inner], gate_up[:, inner:]
                sig = jax.nn.sigmoid(gate)
                gate_grad = hidden_grad * up * sig * (1.0 + gate * (1.0 - sig))
                both[at : at + rows, :inner] = gate_grad.astype(BF16)
                both[at : at + rows, inner:] = (hidden_grad * (gate * sig)).astype(BF16)

        got = lax.dot_general(
            both[...],
            w_ref[0, tile_at(tile, width), :],
            (((1,), (1,)), ((), ())),
            preferred_element_type=F32,
        ).astype(BF16)
        near_out[:, :slots, :] = ahead_ref[...]
        near_out[:, slots:, :] = got[:rows].reshape(peers, slots, tile)
        far_out[:, :slots, :] = got[rows:].reshape(peers, slots, tile)
        far_out[:, slots:, :] = tail_ref[...]

    return run(
        body,
        [jax.ShapeDtypeStruct((peers, 2 * slots, width), BF16)] * 2,
        (width // tile,),
        [fixed(p.shape) for p in (*grad_parts, *near, *far)] + [IN_VMEM, block, block],
        [blocks, blocks],
        [*grad_parts, *near, *far, weight, ahead, tail],
        [pltpu.VMEM((2 * rows, 2 * inner), BF16)],
        deps,
    )


def give(back, group, slots, matrices, more=None, deps=()):
    peers, _, width = back.shape
    count = matrices[0].shape[0]
    tile = wide_tile_of(width)
    column = pl.BlockSpec((count, tile), lambda c: (0, c))

    def body(back_ref, *refs):
        data = back_ref[...].reshape(peers * slots, tile)
        result = jnp.dot(refs[0][...], data, preferred_element_type=F32)
        for ref in refs[1 : len(matrices)]:
            result = result + jnp.dot(ref[...], data, preferred_element_type=F32)
        if more is not None:
            result = result + refs[len(matrices)][...].astype(F32)
        refs[-1][...] = result.astype(BF16)

    return run(
        body,
        jax.ShapeDtypeStruct((count, width), BF16),
        (width // tile,),
        [pl.BlockSpec((peers, slots, tile), lambda c: (0, group, c))]
        + [fixed(m.shape) for m in matrices]
        + ([column] if more is not None else []),
        column,
        [back] + list(matrices) + ([more] if more is not None else []),
        deps=deps,
    )


def finish(back, slots, weighted, plain, out_from, dx_from, deps=()):
    peers, _, width = back.shape
    count = plain.shape[0]
    tile = wide_tile_of(width)
    column = pl.BlockSpec((count, tile), lambda c: (0, c))

    def body(back_ref, high, low, plain_ref, out_ref, dx_ref, layer_out, token_grad):
        rows = [back_ref[:, at : at + slots, :].reshape(peers * slots, tile) for at in (0, slots)]
        result = jnp.dot(high[...], rows[0], preferred_element_type=F32)
        result = result + jnp.dot(low[...], rows[0], preferred_element_type=F32)
        layer_out[...] = (result + out_ref[...].astype(F32)).astype(BF16)
        result = jnp.dot(plain_ref[...], rows[1], preferred_element_type=F32)
        token_grad[...] = (result + dx_ref[...].astype(F32)).astype(BF16)

    return run(
        body,
        [jax.ShapeDtypeStruct((count, width), BF16)] * 2,
        (width // tile,),
        [pl.BlockSpec((peers, 2 * slots, tile), lambda c: (0, 0, c))]
        + [fixed(plain.shape)] * 3
        + [column] * 2,
        [column] * 2,
        [back, *weighted, plain, out_from, dx_from],
        deps=deps,
    )


def expert_grad(where, hidden, far_shares, own, there, slots, deps=()):
    n = len(far_shares)
    peers, _, width = own.shape
    rows = peers * slots
    inner = hidden.shape[1]
    share = inner // n
    tile = wide_tile_of(width)

    def body(where_ref, hidden_ref, *refs):
        share_refs = refs[:n]
        own_ref, there_0, there_1 = refs[n : n + 3]
        out, left = refs[-2:]
        moved = where_ref[1] != 0

        @pl.when(pl.program_id(1) == 0)
        def _():
            @pl.when(jnp.logical_not(moved))
            def _():
                left[...] = hidden_ref[...].astype(F32).T.astype(BF16)

            for d in range(n):
                @pl.when(jnp.logical_and(moved, pl.program_id(0) == d))
                def _():
                    left[...] = share_refs[d][...].astype(F32).T.astype(BF16)

        mine = [own_ref[:, at : at + slots, :].reshape(rows, tile) for at in (0, slots)]
        other = [there_0[...].reshape(rows, tile), there_1[...].reshape(rows, tile)]
        right = [jnp.where(moved, a, b) for a, b in zip(other, mine)]
        got = jnp.dot(left[...], jnp.concatenate(right, axis=0), preferred_element_type=F32)
        out[0] = got.astype(BF16)

    def place(d, where):
        return lax.rem(where[0] - d + n, n)

    return pl.pallas_call(
        body,
        out_shape=pltpu.HBM((1, inner, width), BF16),
        grid_spec=pltpu.PrefetchScalarGridSpec(
            num_scalar_prefetch=1,
            grid=(n, width // tile),
            in_specs=[pl.BlockSpec((2 * rows, share), lambda d, c, w: (0, place(d, w)))]
            + [pl.BlockSpec((2 * rows, share), lambda d, c, w: (0, 0))] * n
            + [pl.BlockSpec((peers, 2 * slots, tile), lambda d, c, w: (0, 0, c))]
            + [pl.BlockSpec((peers, slots, tile), lambda d, c, w: (0, 1, c))] * 2
            + [ANYWHERE] * len(deps),
            out_specs=pl.BlockSpec((1, share, tile), lambda d, c, w: (0, place(d, w), c)),
            scratch_shapes=[pltpu.VMEM((share, 2 * rows), BF16)],
        ),
        cost_estimate=pl.CostEstimate(flops=0, bytes_accessed=0, transcendentals=0),
        compiler_params=pltpu.CompilerParams(vmem_limit_bytes=52 * 1024 * 1024),
    )(where, hidden, *far_shares, own, *there, *deps)


def crossed(block, axis, distance):
    size = lax.axis_size(axis)
    return lax.ppermute(block, axis, [(i, (i + distance) % size) for i in range(size)])


def over_dp(part):
    parts = [part] + [crossed(part, "dp", d) for d in range(1, lax.axis_size("dp"))]
    if len(parts) > 2:
        parts = [sum(p.astype(F32) for p in parts)]
    return parts


def dispatch(routes, weights, firsts, peers, slots, sends, deps=(), flops=0):
    top_count, count = routes.shape
    rows = peers * slots
    ids = jnp.stack(firsts)
    data = [d for send in sends for _, d, _ in send]

    def body(ids_ref, routes_ref, weights_ref, *refs):
        data_refs, outs = list(refs[: len(data)]), list(refs[len(data) :])
        earlier = lax.broadcasted_iota(jnp.int32, (count, count), 0)
        later = lax.broadcasted_iota(jnp.int32, (count, count), 1)
        before = (earlier < later).astype(F32).astype(BF16)
        chosen = []
        for n in range(len(firsts)):
            expert = ids_ref[n] + lax.broadcasted_iota(jnp.int32, (peers, count), 0)
            member = jnp.zeros((peers, count), F32)
            table = jnp.zeros((peers, count), F32)
            for k in range(top_count):
                named = routes_ref[k : k + 1, :] == expert
                member = jnp.where(named, 1.0, member)
                table = jnp.where(named, weights_ref[k : k + 1, :], table)
            place = jnp.dot(member.astype(BF16), before, preferred_element_type=F32)
            place = jnp.where(member > 0.0, place, -1.0)
            slot = lax.broadcasted_iota(jnp.int32, (slots, count), 0).astype(F32)
            hits, weighted = [], []
            for e in range(peers):
                hit = slot == place[e : e + 1, :]
                hits.append(jnp.where(hit, 1.0, 0.0))
                weighted.append(jnp.where(hit, table[e : e + 1, :], 0.0))
            sel = jnp.concatenate(hits, axis=0)
            weighted = jnp.concatenate(weighted, axis=0)
            chosen.append((sel.astype(BF16), jnp.sum(weighted, axis=1, keepdims=True)))
            outs.pop(0)[...] = chosen[-1][0]
            outs.pop(0)[...] = chosen[-1][1]
            if n == 0:
                turned = weighted.T
                high = turned.astype(BF16)
                outs.pop(0)[...] = sel.T.astype(BF16)
                outs.pop(0)[...] = high
                outs.pop(0)[...] = (turned - high.astype(F32)).astype(BF16)
        for send in sends:
            out = outs.pop(0)
            for g, (n, _, weighted) in enumerate(send):
                sel, weight = chosen[n]
                got = jnp.dot(sel, data_refs.pop(0)[...], preferred_element_type=F32)
                if weighted:
                    got = got * weight
                got = got.astype(BF16).reshape(peers, slots, got.shape[1])
                out[:, g * slots : (g + 1) * slots, :] = got

    shapes = []
    for n in range(len(firsts)):
        shapes += [((rows, count), BF16), ((rows, 1), F32)]
        if n == 0:
            shapes += [((count, rows), BF16)] * 3
    for send in sends:
        shapes.append(((peers, slots * len(send), send[0][1].shape[1]), BF16))
    operands = [routes, weights] + data
    out = run(
        body,
        [jax.ShapeDtypeStruct(*shape) for shape in shapes],
        (1,),
        [pl.BlockSpec(memory_space=pltpu.SMEM)] + [fixed(x.shape) for x in operands],
        [fixed(shape) for shape, _ in shapes],
        [ids] + operands,
        deps=deps,
        flops=flops,
    )
    out = list(out)
    result = []
    for n in range(len(firsts)):
        size = 5 if n == 0 else 2
        result.append(out[:size])
        out = out[size:]
    return result, out


def on_device(tokens, out_grad, gate_up_weight, down_weight, routes, route_weight, swapped):
    experts = lax.axis_size("expert")
    half = experts // 2
    token_count = tokens.shape[0]
    top_count = routes.shape[1]
    n_dp = lax.axis_size("dp")
    slots = max(16, 2 * token_count * top_count // experts)
    me = lax.axis_index("expert")
    core = lax.axis_index("dp")
    moved = jnp.any(swapped == me % half)
    here = (me // half) * half
    there = half - here
    groups = [[s * half + j for j in range(half)] for s in range(2)]

    def cross(x):
        return crossed(x, "expert", half)

    def exchange(x):
        return lax.all_to_all(
            x, "expert", split_axis=0, concat_axis=0, tiled=True, axis_index_groups=groups
        )

    routes, route_weight = routes.T, route_weight.T
    tokens_far = cross(tokens)
    routes_far = cross(routes)
    weight_far = cross(route_weight)
    core_at = core.astype(jnp.int32).reshape(1)
    where = jnp.stack([core.astype(jnp.int32), moved.astype(jnp.int32)])

    (near, near_there), (send_1,) = dispatch(
        routes, route_weight, [here, there], half, slots, [[(0, tokens, False)]]
    )
    sel_n, row_n, back_sel_n, *back_wt_n = near
    first = exchange(send_1)
    gate_up_vmem = gate_up_weight
    down_vmem = down_weight

    grad_far = cross(held(out_grad, tokens_far))
    (far, far_there), (send_2,) = dispatch(
        routes_far,
        weight_far,
        [here, there],
        half,
        slots,
        [[(0, tokens_far, False)]],
        deps=(send_1,),
        flops=LONG,
    )
    sel_f, row_f, back_sel_f, *back_wt_f = far
    send_2 = tied(send_2, first)
    second = exchange(send_2)
    part_n = gate_up_part(first, 0, slots, gate_up_vmem, deps=(send_2,))
    parts_n = over_dp(part_n)
    grads_there_n = pick([(near_there[0], out_grad, near_there[1])], half, deps=(part_n,))

    send_3 = pick(
        [(sel_n, out_grad, row_n), (sel_f, grad_far, row_f)],
        half,
        deps=(grads_there_n,),
        flops=LONG,
    )
    send_3 = tied(send_3, second)
    third = exchange(send_3)
    part_f = gate_up_part(second, 0, slots, gate_up_vmem, deps=(send_3,))
    parts_f = over_dp(part_f)
    grads_there_f = pick([(far_there[0], grad_far, far_there[1])], half, deps=(part_f,))
    hidden, share, send_4, out_n = hidden_and_out(
        parts_n, parts_f, down_vmem, core_at, n_dp, half, grads_there_f
    )
    far_share = cross(share)
    send_4 = tied(send_4, third)
    fourth = exchange(send_4)

    grad_parts = over_dp(hidden_grad_part(third, slots, down_vmem, deps=(send_4,)))
    send_5, send_6 = rows_dx(
        grad_parts, parts_n, parts_f, gate_up_vmem, half, out_n, grads_there_n
    )
    send_5 = tied(send_5, fourth, far_share)
    fifth = exchange(send_5)
    far_shares = [far_share] + [crossed(far_share, "dp", d) for d in range(1, n_dp)]
    give_out = give(fourth, 0, slots, back_wt_f, deps=(send_5,))
    out_from = cross(give_out)

    send_6 = tied(send_6, fifth, out_from)
    sixth = exchange(send_6)
    give_dx = give(fifth, 0, slots, [back_sel_f], deps=(send_6,))
    dx_from = cross(give_dx)
    down_grad = expert_grad(
        where, hidden, far_shares, third, (fourth, fifth), slots, deps=(give_dx,)
    )
    layer_out, token_grad = finish(
        sixth, slots, back_wt_n, back_sel_n, out_from, dx_from, deps=(down_grad,)
    )
    return layer_out, token_grad, down_grad


def solution(mesh):
    return jax.shard_map(
        on_device,
        mesh=mesh,
        in_specs=(
            P("expert", "dp"),
            P("expert", "dp"),
            P("expert", "dp", None),
            P("expert", None, "dp"),
            P("expert", None),
            P("expert", None),
            P(),
        ),
        out_specs=(P("expert", "dp"), P("expert", "dp"), P("expert", None, "dp")),
        check_vma=False,
    )
```

```python
import jax
import jax.numpy as jnp
from jax import lax
from jax.experimental import pallas as pl
from jax.experimental.pallas import tpu as pltpu
from jax.sharding import PartitionSpec as P

BF16 = jnp.bfloat16
F32 = jnp.float32
LONG = 50_000_000_000
ANYWHERE = pl.BlockSpec(memory_space=pl.ANY)
IN_VMEM = pl.BlockSpec(memory_space=pltpu.VMEM)


def tile_of(size):
    return 256 if size % 256 == 0 else size


def wide_tile_of(size):
    return size // 2 if size % 256 == 0 else size


def run(body, out_shape, grid, in_specs, out_specs, operands, scratch=(), deps=(), aliases=None, flops=0):
    count = len(operands)
    out_shape = jax.tree.map(
        lambda x: pltpu.HBM(x.shape, x.dtype) if isinstance(x, jax.ShapeDtypeStruct) else x,
        out_shape,
        is_leaf=lambda x: not isinstance(x, (list, tuple)),
    )

    def whole(*refs):
        body(*refs[:count], *refs[count + len(deps) :])

    return pl.pallas_call(
        whole,
        out_shape=out_shape,
        grid=grid,
        in_specs=list(in_specs) + [ANYWHERE] * len(deps),
        out_specs=out_specs,
        scratch_shapes=list(scratch),
        input_output_aliases=aliases or {},
        cost_estimate=pl.CostEstimate(flops=flops, bytes_accessed=0, transcendentals=0),
        compiler_params=pltpu.CompilerParams(vmem_limit_bytes=52 * 1024 * 1024),
    )(*operands, *deps)


def tied(value, *deps, flops=0):
    shape = jax.ShapeDtypeStruct(value.shape, value.dtype)
    return run(lambda *refs: None, shape, (), [ANYWHERE], ANYWHERE, [value], (), deps, {0: 0}, flops)


def held(value, *deps):
    def body(value_ref, out):
        out[...] = value_ref[...]

    rows, width = value.shape
    block = pl.BlockSpec((rows, wide_tile_of(width)), lambda c: (0, c))
    shape = jax.ShapeDtypeStruct(value.shape, value.dtype)
    return run(body, shape, (width // wide_tile_of(width),), [block], block, [value], (), deps)


def fixed(shape):
    return pl.BlockSpec(shape, lambda *at: (0,) * len(shape))


def streamed(shape, tile, dim):
    pieces = shape[dim] // tile
    piece = tuple(tile if d == dim else shape[d] for d in (1, 2))
    return [pltpu.VMEM((pieces,) + piece, BF16), pltpu.SemaphoreType.DMA((pieces,))]


def piece_of(w_ref, held, sems, dim):
    pieces, tile = held.shape[0], held.shape[dim]

    def copy(n):
        at = pl.ds(n * tile, tile)
        source = w_ref.at[0, at, :] if dim == 1 else w_ref.at[0, :, at]
        return pltpu.make_async_copy(source, held.at[n], sems.at[n])

    @pl.when(pl.program_id(0) == 0)
    def _():
        for n in range(pieces):
            copy(n).start()

    def arrived():
        for n in range(pieces):

            @pl.when(pl.program_id(0) == n)
            def _():
                copy(n).wait()

        return held[pl.program_id(0)]

    return arrived


def gate_up_part(x, group, slots, weight, deps=()):
    peers, _, width = x.shape
    rows, columns = peers * slots, weight.shape[2]
    tile = tile_of(columns // 2) * 2

    def body(x_ref, w_ref, out, *scratch):
        piece = piece_of(w_ref, *scratch, 2)
        got = jnp.dot(x_ref[...].reshape(rows, width), piece(), preferred_element_type=F32)
        out[...] = got.astype(BF16)

    return run(
        body,
        jax.ShapeDtypeStruct((rows, columns), BF16),
        (columns // tile,),
        [
            pl.BlockSpec((peers, slots, width), lambda c: (0, group, 0)),
            ANYWHERE,
        ],
        pl.BlockSpec((rows, tile), lambda c: (0, c)),
        [x, weight],
        streamed(weight.shape, tile, 2),
        deps=deps,
    )


def total(refs):
    result = refs[0][...].astype(F32)
    for ref in refs[1:]:
        result = result + ref[...].astype(F32)
    return result


def hidden_and_out(near, far, weight, core, n_dp, peers, deps=()):
    n = len(near)
    rows = near[0].shape[0]
    _, inner, width = weight.shape
    slots = rows // peers
    share = inner // n_dp
    tile = wide_tile_of(width)

    def body(*refs):
        near_refs, far_refs = refs[:n], refs[n : 2 * n]
        core_ref, w_ref, hidden, mine, send, *scratch = refs[2 * n :]
        piece = piece_of(w_ref, *scratch, 2)

        @pl.when(pl.program_id(0) == 0)
        def _():
            for at, part_refs in ((0, near_refs), (rows, far_refs)):
                gate_up = total(part_refs)
                gate = gate_up[:, :inner]
                hidden[at : at + rows, :] = (
                    gate * jax.nn.sigmoid(gate) * gate_up[:, inner:]
                ).astype(BF16)
            first = pl.multiple_of(core_ref[0] * share, 128)
            mine[...] = hidden[:, pl.ds(first, share)]

        got = jnp.dot(hidden[...], piece(), preferred_element_type=F32).astype(BF16)
        send[:, :slots, :] = got[rows:].reshape(peers, slots, tile)
        send[:, slots:, :] = got[:rows].reshape(peers, slots, tile)

    return run(
        body,
        (
            jax.ShapeDtypeStruct((2 * rows, inner), BF16),
            jax.ShapeDtypeStruct((2 * rows, share), BF16),
            jax.ShapeDtypeStruct((peers, 2 * slots, width), BF16),
        ),
        (width // tile,),
        [fixed(p.shape) for p in (*near, *far)]
        + [pl.BlockSpec(memory_space=pltpu.SMEM), ANYWHERE],
        (
            fixed((2 * rows, inner)),
            fixed((2 * rows, share)),
            pl.BlockSpec((peers, 2 * slots, tile), lambda c: (0, 0, c)),
        ),
        [*near, *far, core, weight],
        streamed(weight.shape, tile, 2),
        deps=deps,
    )


def place_rows(pieces, place, slots, out, first):
    peers = len(pieces)
    for d, piece in enumerate(pieces):
        for b in range(2):
            at = pl.multiple_of(first + (b * peers + (place ^ d)) * slots, slots)
            out[pl.ds(at, slots), :] = piece[b * slots : (b + 1) * slots, :]


def hidden_grad_part(scalars, near, far, slots, weight, deps=(), flops=0):
    peers = len(near)
    width = near[0].shape[1]
    inner = weight.shape[1]
    rows = 2 * peers * slots
    tile = tile_of(inner)

    def body(scalar_ref, *refs):
        near_refs, far_refs = refs[:peers], refs[peers : 2 * peers]
        w_ref, out, x, *scratch = refs[2 * peers :]
        piece = piece_of(w_ref, *scratch, 1)

        @pl.when(pl.program_id(0) == 0)
        def _():
            place_rows(near_refs, scalar_ref[3], slots, x, 0)
            place_rows(far_refs, scalar_ref[3], slots, x, rows)

        got = lax.dot_general(
            x[...], piece(), (((1,), (1,)), ((), ())), preferred_element_type=F32
        )
        out[...] = got.astype(BF16)

    return run(
        body,
        [
            jax.ShapeDtypeStruct((2 * rows, inner), BF16),
            jax.ShapeDtypeStruct((2 * rows, width), BF16),
        ],
        (inner // tile,),
        [pl.BlockSpec(memory_space=pltpu.SMEM)]
        + [fixed((2 * slots, width))] * (2 * peers)
        + [ANYWHERE],
        [pl.BlockSpec((2 * rows, tile), lambda c: (0, c)), fixed((2 * rows, width))],
        [scalars, *near, *far, weight],
        streamed(weight.shape, tile, 1),
        deps,
        flops=flops,
    )


def rows_dx(grad_parts, near, far, weight, peers, deps=()):
    n = len(near)
    rows = near[0].shape[0]
    inner = grad_parts[0].shape[1]
    width = weight.shape[1]
    slots = rows // peers
    tile = tile_of(width)
    blocks = pl.BlockSpec((peers, 2 * slots, tile), lambda c: (0, 0, c))

    def body(*refs):
        grad_refs, near_refs, far_refs = refs[:n], refs[n : 2 * n], refs[2 * n : 3 * n]
        w_ref, out, both, *scratch = refs[3 * n :]
        piece = piece_of(w_ref, *scratch, 1)

        @pl.when(pl.program_id(0) == 0)
        def _():
            for at, part_refs in ((0, near_refs), (rows, far_refs)):
                hidden_grad = total([g.at[at : at + rows, :] for g in grad_refs])
                gate_up = total(part_refs)
                gate, up = gate_up[:, :inner], gate_up[:, inner:]
                sig = jax.nn.sigmoid(gate)
                gate_grad = hidden_grad * up * sig * (1.0 + gate * (1.0 - sig))
                both[at : at + rows, :inner] = gate_grad.astype(BF16)
                both[at : at + rows, inner:] = (hidden_grad * (gate * sig)).astype(BF16)

        got = lax.dot_general(
            both[...],
            piece(),
            (((1,), (1,)), ((), ())),
            preferred_element_type=F32,
        ).astype(BF16)
        out[:, :slots, :] = got[rows:].reshape(peers, slots, tile)
        out[:, slots:, :] = got[:rows].reshape(peers, slots, tile)

    return run(
        body,
        jax.ShapeDtypeStruct((peers, 2 * slots, width), BF16),
        (width // tile,),
        [fixed(p.shape) for p in (*grad_parts, *near, *far)] + [ANYWHERE],
        blocks,
        [*grad_parts, *near, *far, weight],
        [pltpu.VMEM((2 * rows, 2 * inner), BF16)] + streamed(weight.shape, tile, 1),
        deps,
    )


def give(back, group, slots, matrices, more=None, deps=()):
    peers, _, width = back.shape
    count = matrices[0].shape[0]
    tile = wide_tile_of(width)
    column = pl.BlockSpec((count, tile), lambda c: (0, c))

    def body(back_ref, *refs):
        data = back_ref[...].reshape(peers * slots, tile)
        result = jnp.dot(refs[0][...], data, preferred_element_type=F32)
        for ref in refs[1 : len(matrices)]:
            result = result + jnp.dot(ref[...], data, preferred_element_type=F32)
        if more is not None:
            result = result + refs[len(matrices)][...].astype(F32)
        refs[-1][...] = result.astype(BF16)

    return run(
        body,
        jax.ShapeDtypeStruct((count, width), BF16),
        (width // tile,),
        [pl.BlockSpec((peers, slots, tile), lambda c: (0, group, c))]
        + [fixed(m.shape) for m in matrices]
        + ([column] if more is not None else []),
        column,
        [back] + list(matrices) + ([more] if more is not None else []),
        deps=deps,
    )


def finish(back_out, back_dx, slots, weighted, plain, out_from, dx_from, deps=()):
    peers, _, width = back_out.shape
    count = plain.shape[0]
    tile = wide_tile_of(width)
    column = pl.BlockSpec((count, tile), lambda c: (0, c))

    def body(back_ref, back_dx_ref, high, low, plain_ref, out_ref, dx_ref, layer_out, token_grad):
        rows = back_ref[...].reshape(peers * slots, tile)
        result = jnp.dot(high[...], rows, preferred_element_type=F32)
        result = result + jnp.dot(low[...], rows, preferred_element_type=F32)
        layer_out[...] = (result + out_ref[...].astype(F32)).astype(BF16)
        rows = back_dx_ref[...].reshape(peers * slots, tile)
        result = jnp.dot(plain_ref[...], rows, preferred_element_type=F32)
        token_grad[...] = (result + dx_ref[...].astype(F32)).astype(BF16)

    return run(
        body,
        [jax.ShapeDtypeStruct((count, width), BF16)] * 2,
        (width // tile,),
        [pl.BlockSpec((peers, slots, tile), lambda c: (0, 1, c))] * 2
        + [fixed(plain.shape)] * 3
        + [column] * 2,
        [column] * 2,
        [back_out, back_dx, *weighted, plain, out_from, dx_from],
        deps=deps,
    )


def expert_grad(where, hidden, far_shares, own, there, slots, deps=(), flops=0):
    n, peers = len(far_shares), len(there)
    rows, width = own.shape
    share = hidden.shape[1] // n
    tile = wide_tile_of(width)

    def body(where_ref, hidden_ref, *refs):
        share_refs, own_ref = refs[:n], refs[n]
        there_refs = refs[n + 1 : n + 1 + peers]
        out, left, right = refs[-3:]
        moved = where_ref[1] != 0
        at = pl.program_id(1)

        @pl.when(pl.program_id(0) == 0)
        def _():
            @pl.when(jnp.logical_not(moved))
            def _():
                left[at] = hidden_ref[...].astype(F32).T.astype(BF16)

            for d in range(n):
                @pl.when(jnp.logical_and(moved, at == d))
                def _():
                    left[at] = share_refs[d][...].astype(F32).T.astype(BF16)

        @pl.when(jnp.logical_and(moved, at == 0))
        def _():
            place_rows([r.at[2 * slots :, :] for r in there_refs], where_ref[2], slots, right, 0)
            place_rows(there_refs, where_ref[2], slots, right, rows // 2)

        @pl.when(jnp.logical_and(jnp.logical_not(moved), at == 0))
        def _():
            right[...] = own_ref[...]

        out[0] = jnp.dot(left[at], right[...], preferred_element_type=F32).astype(BF16)

    def place(d, where):
        return lax.rem(where[0] - d + n, n)

    return pl.pallas_call(
        body,
        out_shape=pltpu.HBM((1, hidden.shape[1], width), BF16),
        grid_spec=pltpu.PrefetchScalarGridSpec(
            num_scalar_prefetch=1,
            grid=(width // tile, n),
            in_specs=[pl.BlockSpec((rows, share), lambda c, d, w: (0, place(d, w)))]
            + [pl.BlockSpec((rows, share), lambda c, d, w: (0, 0))] * n
            + [pl.BlockSpec((rows, tile), lambda c, d, w: (0, c))]
            + [pl.BlockSpec((4 * slots, tile), lambda c, d, w: (0, c))] * peers
            + [ANYWHERE] * len(deps),
            out_specs=pl.BlockSpec((1, share, tile), lambda c, d, w: (0, place(d, w), c)),
            scratch_shapes=[pltpu.VMEM((n, share, rows), BF16), pltpu.VMEM((rows, tile), BF16)],
        ),
        cost_estimate=pl.CostEstimate(flops=flops, bytes_accessed=0, transcendentals=0),
        compiler_params=pltpu.CompilerParams(vmem_limit_bytes=52 * 1024 * 1024),
    )(where, hidden, *far_shares, own, *there, *deps)


def crossed(block, axis, distance):
    size = lax.axis_size(axis)
    return lax.ppermute(block, axis, [(i, (i + distance) % size) for i in range(size)])


def over_dp(part):
    parts = [part] + [crossed(part, "dp", d) for d in range(1, lax.axis_size("dp"))]
    if len(parts) > 2:
        parts = [sum(p.astype(F32) for p in parts)]
    return parts


def chosen(routes, weights, expert, slots):
    count = routes[0].shape[1]
    earlier = lax.broadcasted_iota(jnp.int32, (count, count), 0)
    later = lax.broadcasted_iota(jnp.int32, (count, count), 1)
    before = (earlier < later).astype(F32).astype(BF16)
    peers = expert.shape[0]
    expert = expert.astype(F32)
    member = jnp.zeros((peers, count), F32)
    table = jnp.zeros((peers, count), F32)
    for route, weight in zip(routes, weights):
        named = route == expert
        member = jnp.where(named, 1.0, member)
        table = jnp.where(named, weight, table)
    place = jnp.dot(member.astype(BF16), before, preferred_element_type=F32)
    place = jnp.where(member > 0.0, place, -1.0)
    slot = lax.broadcasted_iota(jnp.int32, (slots, count), 0).astype(F32)
    hits = [slot == place[e : e + 1, :] for e in range(peers)]
    sel = jnp.concatenate([jnp.where(hit, 1.0, 0.0) for hit in hits], axis=0)
    weighted = [jnp.where(hit, table[e : e + 1, :], 0.0) for e, hit in enumerate(hits)]
    return sel, jnp.concatenate(weighted, axis=0)


def dispatch_tokens(table, first, peers, slots, tokens, deps=(), flops=0):
    count, width = tokens.shape
    top_count = table.shape[0] // 2
    rows = peers * slots

    def body(first_ref, table_ref, tokens_ref, send, plain, high, low):
        names = [table_ref[k : k + 1, :] for k in range(2 * top_count)]
        expert = first_ref[0] + lax.broadcasted_iota(jnp.int32, (peers, count), 0)
        sel, weighted = chosen(names[:top_count], names[top_count:], expert, slots)
        got = jnp.dot(sel.astype(BF16), tokens_ref[...], preferred_element_type=F32)
        send[...] = got.astype(BF16).reshape(peers, slots, width)
        plain[...] = sel.T.astype(BF16)
        turned = weighted.T
        top = turned.astype(BF16)
        high[...] = top
        low[...] = (turned - top.astype(F32)).astype(BF16)

    shapes = [((peers, slots, width), BF16)] + [((count, rows), BF16)] * 3
    return run(
        body,
        [jax.ShapeDtypeStruct(*shape) for shape in shapes],
        (1,),
        [pl.BlockSpec(memory_space=pltpu.SMEM), fixed(table.shape), fixed(tokens.shape)],
        [fixed(shape) for shape, _ in shapes],
        [first, table, tokens],
        deps=deps,
        flops=flops,
    )


def dispatch_grads(scalars, table, table_next, own, beside, peers, slots, into=None, deps=(), flops=0):
    top_count = table.shape[0] // 2
    count, width = own.shape

    def body(scalar_ref, table_ref, next_ref, own_ref, beside_ref, *refs):
        *outs, data, names = refs[len(into or ()) :]
        for swap in (0, 1):

            @pl.when(scalar_ref[2] == swap)
            def _():
                for m in range(2):
                    data[m] = (own_ref, beside_ref)[m ^ swap][...]
                    names[m] = (table_ref, next_ref)[m ^ swap][...]

        place = lax.broadcasted_iota(jnp.int32, (peers, count), 0) ^ scalar_ref[3]
        for b in range(2):
            route = [names[b, k : k + 1, :] for k in range(top_count)]
            weight = [names[b, top_count + k : top_count + k + 1, :] for k in range(top_count)]
            for trade in (0, 1):
                sel, weighted = chosen(route, weight, scalar_ref[trade] + place, slots)
                got = jnp.dot(sel.astype(BF16), data[b], preferred_element_type=F32)
                got = (got * jnp.sum(weighted, axis=1, keepdims=True)).astype(BF16)
                for d in range(peers):
                    out = outs[trade * peers + d]
                    out[b * slots : (b + 1) * slots, :] = got[d * slots : (d + 1) * slots, :]

    operands = [scalars, table, table_next, own, beside]
    specs = [pl.BlockSpec(memory_space=pltpu.SMEM)] + [fixed(x.shape) for x in operands[1:]]
    part = 0 if into is None else 1
    aliases = {len(operands) + d: peers + d for d in range(peers * part)}
    out = run(
        body,
        [jax.ShapeDtypeStruct((2 * slots, width), BF16)] * peers
        + [jax.ShapeDtypeStruct((4 * slots, width), BF16)] * peers,
        (1,),
        specs + [ANYWHERE] * (peers * part),
        [fixed((2 * slots, width))] * peers
        + [pl.BlockSpec((2 * slots, width), lambda c: (part, 0))] * peers,
        operands + list(into or ()),
        [pltpu.VMEM((2, count, width), BF16), pltpu.VMEM((2, 2 * top_count, count), F32)],
        deps,
        aliases,
        flops,
    )
    return out[:peers], out[peers:]


def on_device(tokens, out_grad, gate_up_weight, down_weight, routes, route_weight, swapped):
    experts = lax.axis_size("expert")
    n_dp = lax.axis_size("dp")
    half, plane = experts // 2, experts // 4
    token_count = tokens.shape[0]
    top_count = routes.shape[1]
    slots = max(16, 2 * token_count * top_count // experts)
    me = lax.axis_index("expert").astype(jnp.int32)
    core = lax.axis_index("dp").astype(jnp.int32)
    moved = jnp.any(swapped == me % half).astype(jnp.int32)
    here = (me // half) * half
    layer = (me // plane) * plane
    halves = [[s * half + j for j in range(half)] for s in range(2)]

    def cross(x):
        return crossed(x, "expert", half)

    def beside(x):
        return lax.ppermute(x, "expert", [(i, i ^ plane) for i in range(experts)])

    def exchange(x):
        return lax.all_to_all(
            x, "expert", split_axis=0, concat_axis=0, tiled=True, axis_index_groups=halves
        )

    def over_plane(pieces):
        return [pieces[0]] + [
            lax.ppermute(pieces[d], "expert", [(i, i ^ d) for i in range(experts)])
            for d in range(1, plane)
        ]

    tokens_far = cross(tokens)
    table = jnp.concatenate([routes.T.astype(F32), route_weight.T], axis=0)
    table_far = cross(table)
    table_beside = beside(table)
    table_corner = lax.ppermute(
        table, "expert", [(i, (i ^ plane) ^ half) for i in range(experts)]
    )
    grad_beside = beside(out_grad)
    first_at = here.reshape(1)
    scalars = jnp.stack([layer, (layer + half) % experts, (me // plane) % 2, me % plane])
    where = jnp.stack([core, moved, me % plane])

    send_1, back_sel_n, *back_wt_n = dispatch_tokens(table, first_at, half, slots, tokens)
    first = exchange(send_1)
    send_near, trade_near = dispatch_grads(
        scalars, table, table_beside, out_grad, grad_beside, plane, slots, deps=(send_1, table_corner)
    )
    grads_near = over_plane(send_near)
    grad_copy = held(out_grad, tokens_far, send_near[0])
    grad_far = cross(grad_copy)
    send_2, back_sel_f, *back_wt_f = dispatch_tokens(
        table_far, first_at, half, slots, tokens_far, deps=(grad_copy,), flops=LONG
    )
    send_2 = tied(send_2, first)
    second = exchange(send_2)
    part_n = gate_up_part(first, 0, slots, gate_up_weight, deps=(send_2,))
    parts_n = over_dp(part_n)
    grad_far = tied(grad_far, part_n, flops=LONG)
    far_beside = beside(grad_far)
    part_f = gate_up_part(second, 0, slots, gate_up_weight, deps=(part_n,))
    parts_f = over_dp(part_f)

    send_far, trade = dispatch_grads(
        scalars,
        table_far,
        table_corner,
        grad_far,
        far_beside,
        plane,
        slots,
        into=trade_near,
        deps=(part_f, *grads_near[1:]),
        flops=LONG,
    )
    grads_far = over_plane(send_far)
    hidden, share, send_4 = hidden_and_out(
        parts_n, parts_f, down_weight, core.reshape(1), n_dp, half, deps=(send_far[0],)
    )
    far_share = cross(share)
    send_4 = tied(send_4, second)
    fourth = exchange(send_4)

    grad_part, grads = hidden_grad_part(
        scalars, grads_near, grads_far, slots, down_weight, deps=(send_4,), flops=LONG
    )
    grad_parts = over_dp(grad_part)
    far_share = tied(far_share, flops=LONG)
    send_5 = rows_dx(grad_parts, parts_n, parts_f, gate_up_weight, half, deps=(far_share,))
    send_5 = tied(send_5, fourth)
    fifth = exchange(send_5)
    far_shares = [far_share] + [crossed(far_share, "dp", d) for d in range(1, n_dp)]
    give_out = give(fourth, 0, slots, back_wt_f, deps=(send_5,))
    out_from = cross(give_out)

    give_dx = give(fifth, 0, slots, [back_sel_f], deps=(out_from,))
    dx_from = cross(give_dx)
    down_grad = expert_grad(
        where, hidden, far_shares, grads, over_plane(trade), slots, deps=(give_dx,)
    )
    layer_out, token_grad = finish(
        fourth, fifth, slots, back_wt_n, back_sel_n, out_from, dx_from, deps=(down_grad,)
    )
    return layer_out, token_grad, down_grad


def solution(mesh):
    return jax.shard_map(
        on_device,
        mesh=mesh,
        in_specs=(
            P("expert", "dp"),
            P("expert", "dp"),
            P("expert", "dp", None),
            P("expert", None, "dp"),
            P("expert", None),
            P("expert", None),
            P(),
        ),
        out_specs=(P("expert", "dp"), P("expert", "dp"), P("expert", None, "dp")),
        check_vma=False,
    )
```

```python
import jax
import jax.numpy as jnp
from jax import lax
from jax.experimental import pallas as pl
from jax.experimental.pallas import tpu as pltpu
from jax.sharding import PartitionSpec as P

BF16 = jnp.bfloat16
F32 = jnp.float32
LONG = 50_000_000_000
PARTS = 4
ANYWHERE = pl.BlockSpec(memory_space=pl.ANY)
IN_VMEM = pl.BlockSpec(memory_space=pltpu.VMEM)


def tile_of(size):
    return 256 if size % 256 == 0 else size


def wide_tile_of(size):
    return size // 2 if size % 256 == 0 else size


def run(body, out_shape, grid, in_specs, out_specs, operands, scratch=(), deps=(), aliases=None, flops=0):
    count = len(operands)
    out_shape = jax.tree.map(
        lambda x: pltpu.HBM(x.shape, x.dtype) if isinstance(x, jax.ShapeDtypeStruct) else x,
        out_shape,
        is_leaf=lambda x: not isinstance(x, (list, tuple)),
    )

    def whole(*refs):
        body(*refs[:count], *refs[count + len(deps) :])

    return pl.pallas_call(
        whole,
        out_shape=out_shape,
        grid=grid,
        in_specs=list(in_specs) + [ANYWHERE] * len(deps),
        out_specs=out_specs,
        scratch_shapes=list(scratch),
        input_output_aliases=aliases or {},
        cost_estimate=pl.CostEstimate(flops=flops, bytes_accessed=0, transcendentals=0),
        compiler_params=pltpu.CompilerParams(vmem_limit_bytes=52 * 1024 * 1024),
    )(*operands, *deps)


def tied(value, *deps, flops=0):
    shape = jax.ShapeDtypeStruct(value.shape, value.dtype)
    return run(lambda *refs: None, shape, (), [ANYWHERE], ANYWHERE, [value], (), deps, {0: 0}, flops)


def held(value, *deps):
    def body(value_ref, out):
        out[...] = value_ref[...]

    rows, width = value.shape
    block = pl.BlockSpec((rows, wide_tile_of(width)), lambda c: (0, c))
    shape = jax.ShapeDtypeStruct(value.shape, value.dtype)
    return run(body, shape, (width // wide_tile_of(width),), [block], block, [value], (), deps)


def fixed(shape):
    return pl.BlockSpec(shape, lambda *at: (0,) * len(shape))


def streamed(shape, tile, dim):
    pieces = shape[dim] // tile
    piece = tuple(tile if d == dim else shape[d] for d in (1, 2))
    return [pltpu.VMEM((pieces,) + piece, BF16), pltpu.SemaphoreType.DMA((pieces,))]


def piece_of(w_ref, held, sems, dim):
    pieces, tile = held.shape[0], held.shape[dim]

    def copy(n):
        at = pl.ds(n * tile, tile)
        source = w_ref.at[0, at, :] if dim == 1 else w_ref.at[0, :, at]
        return pltpu.make_async_copy(source, held.at[n], sems.at[n])

    @pl.when(pl.program_id(0) == 0)
    def _():
        for n in range(pieces):
            copy(n).start()

    def arrived():
        for n in range(pieces):

            @pl.when(pl.program_id(0) == n)
            def _():
                copy(n).wait()

        return held[pl.program_id(0)]

    return arrived


def gate_up_part(x, group, slots, weight, deps=()):
    peers, _, width = x.shape
    rows, columns = peers * slots, weight.shape[2]
    tile = tile_of(columns // 2) * 2

    def body(x_ref, w_ref, out, *scratch):
        piece = piece_of(w_ref, *scratch, 2)
        got = jnp.dot(x_ref[...].reshape(rows, width), piece(), preferred_element_type=F32)
        out[...] = got.astype(BF16)

    return run(
        body,
        jax.ShapeDtypeStruct((rows, columns), BF16),
        (columns // tile,),
        [
            pl.BlockSpec((peers, slots, width), lambda c: (0, group, 0)),
            ANYWHERE,
        ],
        pl.BlockSpec((rows, tile), lambda c: (0, c)),
        [x, weight],
        streamed(weight.shape, tile, 2),
        deps=deps,
    )


def total(refs):
    result = refs[0][...].astype(F32)
    for ref in refs[1:]:
        result = result + ref[...].astype(F32)
    return result


def hidden_and_out(near, far, weight, core, n_dp, peers, deps=()):
    n = len(near)
    rows = near[0].shape[0]
    _, inner, width = weight.shape
    slots = rows // peers
    share = inner // n_dp
    tile = wide_tile_of(width)

    def body(*refs):
        near_refs, far_refs = refs[:n], refs[n : 2 * n]
        core_ref, w_ref, hidden, mine, send, *scratch = refs[2 * n :]
        piece = piece_of(w_ref, *scratch, 2)

        @pl.when(pl.program_id(0) == 0)
        def _():
            for at, part_refs in ((0, near_refs), (rows, far_refs)):
                gate_up = total(part_refs)
                gate = gate_up[:, :inner]
                hidden[at : at + rows, :] = (
                    gate * jax.nn.sigmoid(gate) * gate_up[:, inner:]
                ).astype(BF16)
            first = pl.multiple_of(core_ref[0] * share, 128)
            mine[...] = hidden[:, pl.ds(first, share)]

        got = jnp.dot(hidden[...], piece(), preferred_element_type=F32).astype(BF16)
        send[:, :slots, :] = got[rows:].reshape(peers, slots, tile)
        send[:, slots:, :] = got[:rows].reshape(peers, slots, tile)

    return run(
        body,
        (
            jax.ShapeDtypeStruct((2 * rows, inner), BF16),
            jax.ShapeDtypeStruct((2 * rows, share), BF16),
            jax.ShapeDtypeStruct((peers, 2 * slots, width), BF16),
        ),
        (width // tile,),
        [fixed(p.shape) for p in (*near, *far)]
        + [pl.BlockSpec(memory_space=pltpu.SMEM), ANYWHERE],
        (
            fixed((2 * rows, inner)),
            fixed((2 * rows, share)),
            pl.BlockSpec((peers, 2 * slots, tile), lambda c: (0, 0, c)),
        ),
        [*near, *far, core, weight],
        streamed(weight.shape, tile, 2),
        deps=deps,
    )


def place_rows(pieces, place, slots, out, first):
    peers = len(pieces)
    for d, piece in enumerate(pieces):
        for b in range(2):
            at = pl.multiple_of(first + (b * peers + (place ^ d)) * slots, slots)
            out[pl.ds(at, slots), :] = piece[b * slots : (b + 1) * slots, :]


def hidden_grad_part(scalars, near, far, slots, weight, deps=(), flops=0):
    peers = len(near)
    width = near[0].shape[1]
    inner = weight.shape[1]
    rows = 2 * peers * slots
    step = 2 * rows // PARTS
    tile = tile_of(inner)

    def body(scalar_ref, *refs):
        near_refs, far_refs = refs[:peers], refs[peers : 2 * peers]
        w_ref, *outs, x = refs[2 * peers : 2 * peers + PARTS + 2]
        scratch = refs[2 * peers + PARTS + 2 :]
        piece = piece_of(w_ref, *scratch, 1)

        @pl.when(pl.program_id(0) == 0)
        def _():
            place_rows(near_refs, scalar_ref[3], slots, x, 0)
            place_rows(far_refs, scalar_ref[3], slots, x, rows)

        got = lax.dot_general(
            x[...], piece(), (((1,), (1,)), ((), ())), preferred_element_type=F32
        )
        for p, out in enumerate(outs):
            out[...] = got[p * step : (p + 1) * step].astype(BF16)

    return run(
        body,
        [jax.ShapeDtypeStruct((step, inner), BF16)] * PARTS
        + [jax.ShapeDtypeStruct((2 * rows, width), BF16)],
        (inner // tile,),
        [pl.BlockSpec(memory_space=pltpu.SMEM)]
        + [fixed((2 * slots, width))] * (2 * peers)
        + [ANYWHERE],
        [pl.BlockSpec((step, tile), lambda c: (0, c))] * PARTS + [fixed((2 * rows, width))],
        [scalars, *near, *far, weight],
        streamed(weight.shape, tile, 1),
        deps,
        flops=flops,
    )


def rows_dx(grad_parts, near, far, weight, peers, deps=()):
    n = len(near)
    rows = near[0].shape[0]
    inner = grad_parts[0][0].shape[1]
    step = 2 * rows // PARTS
    width = weight.shape[1]
    slots = rows // peers
    tile = tile_of(width)
    blocks = pl.BlockSpec((peers, 2 * slots, tile), lambda c: (0, 0, c))

    def body(*refs):
        grad_refs, refs = refs[: PARTS * n], refs[PARTS * n :]
        near_refs, far_refs = refs[:n], refs[n : 2 * n]
        w_ref, out, both, *scratch = refs[2 * n :]
        piece = piece_of(w_ref, *scratch, 1)

        @pl.when(pl.program_id(0) == 0)
        def _():
            for p in range(PARTS):
                hidden_grad = total(grad_refs[p * n : (p + 1) * n])
                part_refs, at = (near_refs, p * step) if p * step < rows else (far_refs, p * step - rows)
                gate_up = total([ref.at[at : at + step, :] for ref in part_refs])
                gate, up = gate_up[:, :inner], gate_up[:, inner:]
                sig = jax.nn.sigmoid(gate)
                gate_grad = hidden_grad * up * sig * (1.0 + gate * (1.0 - sig))
                both[p * step : (p + 1) * step, :inner] = gate_grad.astype(BF16)
                both[p * step : (p + 1) * step, inner:] = (hidden_grad * (gate * sig)).astype(BF16)

        got = lax.dot_general(
            both[...],
            piece(),
            (((1,), (1,)), ((), ())),
            preferred_element_type=F32,
        ).astype(BF16)
        out[:, :slots, :] = got[rows:].reshape(peers, slots, tile)
        out[:, slots:, :] = got[:rows].reshape(peers, slots, tile)

    return run(
        body,
        jax.ShapeDtypeStruct((peers, 2 * slots, width), BF16),
        (width // tile,),
        [fixed(p.shape) for p in (*sum(grad_parts, []), *near, *far)] + [ANYWHERE],
        blocks,
        [*sum(grad_parts, []), *near, *far, weight],
        [pltpu.VMEM((2 * rows, 2 * inner), BF16)] + streamed(weight.shape, tile, 1),
        deps,
    )


def give(back, group, slots, matrices, more=None, deps=()):
    peers, _, width = back.shape
    count = matrices[0].shape[0]
    tile = wide_tile_of(width)
    column = pl.BlockSpec((count, tile), lambda c: (0, c))

    def body(back_ref, *refs):
        data = back_ref[...].reshape(peers * slots, tile)
        result = jnp.dot(refs[0][...], data, preferred_element_type=F32)
        for ref in refs[1 : len(matrices)]:
            result = result + jnp.dot(ref[...], data, preferred_element_type=F32)
        if more is not None:
            result = result + refs[len(matrices)][...].astype(F32)
        refs[-1][...] = result.astype(BF16)

    return run(
        body,
        jax.ShapeDtypeStruct((count, width), BF16),
        (width // tile,),
        [pl.BlockSpec((peers, slots, tile), lambda c: (0, group, c))]
        + [fixed(m.shape) for m in matrices]
        + ([column] if more is not None else []),
        column,
        [back] + list(matrices) + ([more] if more is not None else []),
        deps=deps,
    )


def finish(back_out, back_dx, slots, weighted, plain, out_from, dx_from, deps=()):
    peers, _, width = back_out.shape
    count = plain.shape[0]
    tile = wide_tile_of(width)
    column = pl.BlockSpec((count, tile), lambda c: (0, c))

    def body(back_ref, back_dx_ref, high, low, plain_ref, out_ref, dx_ref, layer_out, token_grad):
        rows = back_ref[...].reshape(peers * slots, tile)
        result = jnp.dot(high[...], rows, preferred_element_type=F32)
        result = result + jnp.dot(low[...], rows, preferred_element_type=F32)
        layer_out[...] = (result + out_ref[...].astype(F32)).astype(BF16)
        rows = back_dx_ref[...].reshape(peers * slots, tile)
        result = jnp.dot(plain_ref[...], rows, preferred_element_type=F32)
        token_grad[...] = (result + dx_ref[...].astype(F32)).astype(BF16)

    return run(
        body,
        [jax.ShapeDtypeStruct((count, width), BF16)] * 2,
        (width // tile,),
        [pl.BlockSpec((peers, slots, tile), lambda c: (0, 1, c))] * 2
        + [fixed(plain.shape)] * 3
        + [column] * 2,
        [column] * 2,
        [back_out, back_dx, *weighted, plain, out_from, dx_from],
        deps=deps,
    )


def expert_grad(where, hidden, far_shares, own, there, slots, deps=(), flops=0):
    n, peers = len(far_shares), len(there)
    rows, width = own.shape
    share = hidden.shape[1] // n
    tile = wide_tile_of(width)

    def body(where_ref, hidden_ref, *refs):
        share_refs, own_ref = refs[:n], refs[n]
        there_refs = refs[n + 1 : n + 1 + peers]
        out, left, right = refs[-3:]
        moved = where_ref[1] != 0
        at = pl.program_id(1)

        @pl.when(pl.program_id(0) == 0)
        def _():
            @pl.when(jnp.logical_not(moved))
            def _():
                left[at] = hidden_ref[...].astype(F32).T.astype(BF16)

            for d in range(n):
                @pl.when(jnp.logical_and(moved, at == d))
                def _():
                    left[at] = share_refs[d][...].astype(F32).T.astype(BF16)

        @pl.when(jnp.logical_and(moved, at == 0))
        def _():
            place_rows([r.at[2 * slots :, :] for r in there_refs], where_ref[2], slots, right, 0)
            place_rows(there_refs, where_ref[2], slots, right, rows // 2)

        @pl.when(jnp.logical_and(jnp.logical_not(moved), at == 0))
        def _():
            right[...] = own_ref[...]

        out[0] = jnp.dot(left[at], right[...], preferred_element_type=F32).astype(BF16)

    def place(d, where):
        return lax.rem(where[0] - d + n, n)

    return pl.pallas_call(
        body,
        out_shape=pltpu.HBM((1, hidden.shape[1], width), BF16),
        grid_spec=pltpu.PrefetchScalarGridSpec(
            num_scalar_prefetch=1,
            grid=(width // tile, n),
            in_specs=[pl.BlockSpec((rows, share), lambda c, d, w: (0, place(d, w)))]
            + [pl.BlockSpec((rows, share), lambda c, d, w: (0, 0))] * n
            + [pl.BlockSpec((rows, tile), lambda c, d, w: (0, c))]
            + [pl.BlockSpec((4 * slots, tile), lambda c, d, w: (0, c))] * peers
            + [ANYWHERE] * len(deps),
            out_specs=pl.BlockSpec((1, share, tile), lambda c, d, w: (0, place(d, w), c)),
            scratch_shapes=[pltpu.VMEM((n, share, rows), BF16), pltpu.VMEM((rows, tile), BF16)],
        ),
        cost_estimate=pl.CostEstimate(flops=flops, bytes_accessed=0, transcendentals=0),
        compiler_params=pltpu.CompilerParams(vmem_limit_bytes=52 * 1024 * 1024),
    )(where, hidden, *far_shares, own, *there, *deps)


def crossed(block, axis, distance):
    size = lax.axis_size(axis)
    return lax.ppermute(block, axis, [(i, (i + distance) % size) for i in range(size)])


def over_dp(part):
    parts = [part] + [crossed(part, "dp", d) for d in range(1, lax.axis_size("dp"))]
    if len(parts) > 2:
        parts = [sum(p.astype(F32) for p in parts)]
    return parts


def chosen(routes, weights, expert, slots):
    count = routes[0].shape[1]
    earlier = lax.broadcasted_iota(jnp.int32, (count, count), 0)
    later = lax.broadcasted_iota(jnp.int32, (count, count), 1)
    before = (earlier < later).astype(F32).astype(BF16)
    peers = expert.shape[0]
    expert = expert.astype(F32)
    member = jnp.zeros((peers, count), F32)
    table = jnp.zeros((peers, count), F32)
    for route, weight in zip(routes, weights):
        named = route == expert
        member = jnp.where(named, 1.0, member)
        table = jnp.where(named, weight, table)
    place = jnp.dot(member.astype(BF16), before, preferred_element_type=F32)
    place = jnp.where(member > 0.0, place, -1.0)
    slot = lax.broadcasted_iota(jnp.int32, (slots, count), 0).astype(F32)
    hits = [slot == place[e : e + 1, :] for e in range(peers)]
    sel = jnp.concatenate([jnp.where(hit, 1.0, 0.0) for hit in hits], axis=0)
    weighted = [jnp.where(hit, table[e : e + 1, :], 0.0) for e, hit in enumerate(hits)]
    return sel, jnp.concatenate(weighted, axis=0)


def dispatch_tokens(table, first, peers, slots, tokens, deps=(), flops=0):
    count, width = tokens.shape
    top_count = table.shape[0] // 2
    rows = peers * slots

    def body(first_ref, table_ref, tokens_ref, send, plain, high, low):
        names = [table_ref[k : k + 1, :] for k in range(2 * top_count)]
        expert = first_ref[0] + lax.broadcasted_iota(jnp.int32, (peers, count), 0)
        sel, weighted = chosen(names[:top_count], names[top_count:], expert, slots)
        got = jnp.dot(sel.astype(BF16), tokens_ref[...], preferred_element_type=F32)
        send[...] = got.astype(BF16).reshape(peers, slots, width)
        plain[...] = sel.T.astype(BF16)
        turned = weighted.T
        top = turned.astype(BF16)
        high[...] = top
        low[...] = (turned - top.astype(F32)).astype(BF16)

    shapes = [((peers, slots, width), BF16)] + [((count, rows), BF16)] * 3
    return run(
        body,
        [jax.ShapeDtypeStruct(*shape) for shape in shapes],
        (1,),
        [pl.BlockSpec(memory_space=pltpu.SMEM), fixed(table.shape), fixed(tokens.shape)],
        [fixed(shape) for shape, _ in shapes],
        [first, table, tokens],
        deps=deps,
        flops=flops,
    )


def dispatch_grads(scalars, table, table_next, own, beside, peers, slots, into=None, deps=(), flops=0):
    top_count = table.shape[0] // 2
    count, width = own.shape

    def body(scalar_ref, table_ref, next_ref, own_ref, beside_ref, *refs):
        *outs, data, names = refs[len(into or ()) :]
        for swap in (0, 1):

            @pl.when(scalar_ref[2] == swap)
            def _():
                for m in range(2):
                    data[m] = (own_ref, beside_ref)[m ^ swap][...]
                    names[m] = (table_ref, next_ref)[m ^ swap][...]

        place = lax.broadcasted_iota(jnp.int32, (peers, count), 0) ^ scalar_ref[3]
        for b in range(2):
            route = [names[b, k : k + 1, :] for k in range(top_count)]
            weight = [names[b, top_count + k : top_count + k + 1, :] for k in range(top_count)]
            for trade in (0, 1):
                sel, weighted = chosen(route, weight, scalar_ref[trade] + place, slots)
                got = jnp.dot(sel.astype(BF16), data[b], preferred_element_type=F32)
                got = (got * jnp.sum(weighted, axis=1, keepdims=True)).astype(BF16)
                for d in range(peers):
                    out = outs[trade * peers + d]
                    out[b * slots : (b + 1) * slots, :] = got[d * slots : (d + 1) * slots, :]

    operands = [scalars, table, table_next, own, beside]
    specs = [pl.BlockSpec(memory_space=pltpu.SMEM)] + [fixed(x.shape) for x in operands[1:]]
    part = 0 if into is None else 1
    aliases = {len(operands) + d: peers + d for d in range(peers * part)}
    out = run(
        body,
        [jax.ShapeDtypeStruct((2 * slots, width), BF16)] * peers
        + [jax.ShapeDtypeStruct((4 * slots, width), BF16)] * peers,
        (1,),
        specs + [ANYWHERE] * (peers * part),
        [fixed((2 * slots, width))] * peers
        + [pl.BlockSpec((2 * slots, width), lambda c: (part, 0))] * peers,
        operands + list(into or ()),
        [pltpu.VMEM((2, count, width), BF16), pltpu.VMEM((2, 2 * top_count, count), F32)],
        deps,
        aliases,
        flops,
    )
    return out[:peers], out[peers:]


def on_device(tokens, out_grad, gate_up_weight, down_weight, routes, route_weight, swapped):
    experts = lax.axis_size("expert")
    n_dp = lax.axis_size("dp")
    half, plane = experts // 2, experts // 4
    token_count = tokens.shape[0]
    top_count = routes.shape[1]
    slots = max(16, 2 * token_count * top_count // experts)
    me = lax.axis_index("expert").astype(jnp.int32)
    core = lax.axis_index("dp").astype(jnp.int32)
    moved = jnp.any(swapped == me % half).astype(jnp.int32)
    here = (me // half) * half
    layer = (me // plane) * plane
    halves = [[s * half + j for j in range(half)] for s in range(2)]

    def cross(x):
        return crossed(x, "expert", half)

    def beside(x):
        return lax.ppermute(x, "expert", [(i, i ^ plane) for i in range(experts)])

    def exchange(x):
        return lax.all_to_all(
            x, "expert", split_axis=0, concat_axis=0, tiled=True, axis_index_groups=halves
        )

    def over_plane(pieces):
        return [pieces[0]] + [
            lax.ppermute(pieces[d], "expert", [(i, i ^ d) for i in range(experts)])
            for d in range(1, plane)
        ]

    tokens_far = cross(tokens)
    table = jnp.concatenate([routes.T.astype(F32), route_weight.T], axis=0)
    table_far = cross(table)
    table_beside = beside(table)
    table_corner = lax.ppermute(
        table, "expert", [(i, (i ^ plane) ^ half) for i in range(experts)]
    )
    grad_beside = beside(out_grad)
    first_at = here.reshape(1)
    scalars = jnp.stack([layer, (layer + half) % experts, (me // plane) % 2, me % plane])
    where = jnp.stack([core, moved, me % plane])

    send_1, back_sel_n, *back_wt_n = dispatch_tokens(table, first_at, half, slots, tokens)
    first = exchange(send_1)
    send_near, trade_near = dispatch_grads(
        scalars, table, table_beside, out_grad, grad_beside, plane, slots, deps=(send_1, table_corner)
    )
    grads_near = over_plane(send_near)
    grad_copy = held(out_grad, tokens_far, send_near[0])
    grad_far = cross(grad_copy)
    send_2, back_sel_f, *back_wt_f = dispatch_tokens(
        table_far, first_at, half, slots, tokens_far, deps=(grad_copy,), flops=LONG
    )
    send_2 = tied(send_2, first)
    second = exchange(send_2)
    part_n = gate_up_part(first, 0, slots, gate_up_weight, deps=(send_2,))
    parts_n = over_dp(part_n)
    grad_far = tied(grad_far, part_n, flops=LONG)
    far_beside = beside(grad_far)
    part_f = gate_up_part(second, 0, slots, gate_up_weight, deps=(part_n,))
    parts_f = over_dp(part_f)

    send_far, trade = dispatch_grads(
        scalars,
        table_far,
        table_corner,
        grad_far,
        far_beside,
        plane,
        slots,
        into=trade_near,
        deps=(part_f, *grads_near[1:]),
        flops=LONG,
    )
    grads_far = over_plane(send_far)
    hidden, share, send_4 = hidden_and_out(
        parts_n, parts_f, down_weight, core.reshape(1), n_dp, half, deps=(send_far[0],)
    )
    far_share = cross(share)
    send_4 = tied(send_4, second)
    fourth = exchange(send_4)

    *grad_part, grads = hidden_grad_part(
        scalars, grads_near, grads_far, slots, down_weight, deps=(send_4,), flops=LONG
    )
    grad_parts = [over_dp(part) for part in grad_part]
    send_5 = rows_dx(grad_parts, parts_n, parts_f, gate_up_weight, half)
    send_5 = tied(send_5, fourth, far_share)
    fifth = exchange(send_5)
    far_shares = [far_share] + [crossed(far_share, "dp", d) for d in range(1, n_dp)]
    give_out = give(fourth, 0, slots, back_wt_f, deps=(send_5,))
    out_from = cross(give_out)

    give_dx = give(fifth, 0, slots, [back_sel_f], deps=(out_from,))
    dx_from = cross(give_dx)
    down_grad = expert_grad(
        where, hidden, far_shares, grads, over_plane(trade), slots, deps=(give_dx,)
    )
    layer_out, token_grad = finish(
        fourth, fifth, slots, back_wt_n, back_sel_n, out_from, dx_from, deps=(down_grad,)
    )
    return layer_out, token_grad, down_grad


def solution(mesh):
    return jax.shard_map(
        on_device,
        mesh=mesh,
        in_specs=(
            P("expert", "dp"),
            P("expert", "dp"),
            P("expert", "dp", None),
            P("expert", None, "dp"),
            P("expert", None),
            P("expert", None),
            P(),
        ),
        out_specs=(P("expert", "dp"), P("expert", "dp"), P("expert", None, "dp")),
        check_vma=False,
    )
```

```python
import jax
import jax.numpy as jnp
from jax import lax
from jax.experimental import pallas as pl
from jax.experimental.pallas import tpu as pltpu
from jax.sharding import PartitionSpec as P

BF16 = jnp.bfloat16
F32 = jnp.float32
LONG = 50_000_000_000
PARTS = 4
ANYWHERE = pl.BlockSpec(memory_space=pl.ANY)
IN_VMEM = pl.BlockSpec(memory_space=pltpu.VMEM)


def tile_of(size):
    return 256 if size % 256 == 0 else size


def wide_tile_of(size):
    return size // 2 if size % 256 == 0 else size


def run(body, out_shape, grid, in_specs, out_specs, operands, scratch=(), deps=(), aliases=None, flops=0):
    count = len(operands)
    out_shape = jax.tree.map(
        lambda x: pltpu.HBM(x.shape, x.dtype) if isinstance(x, jax.ShapeDtypeStruct) else x,
        out_shape,
        is_leaf=lambda x: not isinstance(x, (list, tuple)),
    )

    def whole(*refs):
        body(*refs[:count], *refs[count + len(deps) :])

    return pl.pallas_call(
        whole,
        out_shape=out_shape,
        grid=grid,
        in_specs=list(in_specs) + [ANYWHERE] * len(deps),
        out_specs=out_specs,
        scratch_shapes=list(scratch),
        input_output_aliases=aliases or {},
        cost_estimate=pl.CostEstimate(flops=flops, bytes_accessed=0, transcendentals=0),
        compiler_params=pltpu.CompilerParams(vmem_limit_bytes=50 * 1024 * 1024),
    )(*operands, *deps)


def tied(value, *deps, flops=0):
    shape = jax.ShapeDtypeStruct(value.shape, value.dtype)
    return run(lambda *refs: None, shape, (), [ANYWHERE], ANYWHERE, [value], (), deps, {0: 0}, flops)


def held(value, *deps):
    def body(value_ref, out):
        out[...] = value_ref[...]

    rows, width = value.shape
    block = pl.BlockSpec((rows, wide_tile_of(width)), lambda c: (0, c))
    shape = jax.ShapeDtypeStruct(value.shape, value.dtype)
    return run(body, shape, (width // wide_tile_of(width),), [block], block, [value], (), deps)


def fixed(shape):
    return pl.BlockSpec(shape, lambda *at: (0,) * len(shape))


def streamed(shape, tile, dim):
    pieces = shape[dim] // tile
    piece = tuple(tile if d == dim else shape[d] for d in (1, 2))
    return [pltpu.VMEM((pieces,) + piece, BF16), pltpu.SemaphoreType.DMA((pieces,))]


def piece_of(w_ref, held, sems, dim):
    pieces, tile = held.shape[0], held.shape[dim]

    def copy(n):
        at = pl.ds(n * tile, tile)
        source = w_ref.at[0, at, :] if dim == 1 else w_ref.at[0, :, at]
        return pltpu.make_async_copy(source, held.at[n], sems.at[n])

    @pl.when(pl.program_id(0) == 0)
    def _():
        for n in range(pieces):
            copy(n).start()

    def arrived():
        for n in range(pieces):

            @pl.when(pl.program_id(0) == n)
            def _():
                copy(n).wait()

        return held[pl.program_id(0)]

    return arrived


def gate_up_part(x, group, slots, weight, deps=()):
    peers, _, width = x.shape
    rows, columns = peers * slots, weight.shape[2]
    tile = tile_of(columns // 2) * 2

    def body(x_ref, w_ref, out, *scratch):
        piece = piece_of(w_ref, *scratch, 2)
        got = jnp.dot(x_ref[...].reshape(rows, width), piece(), preferred_element_type=F32)
        out[...] = got.astype(BF16)

    return run(
        body,
        jax.ShapeDtypeStruct((rows, columns), BF16),
        (columns // tile,),
        [
            pl.BlockSpec((peers, slots, width), lambda c: (0, group, 0)),
            ANYWHERE,
        ],
        pl.BlockSpec((rows, tile), lambda c: (0, c)),
        [x, weight],
        streamed(weight.shape, tile, 2),
        deps=deps,
    )


def total(refs):
    result = refs[0][...].astype(F32)
    for ref in refs[1:]:
        result = result + ref[...].astype(F32)
    return result


def hidden_and_out(near, far, weight, core, n_dp, peers, deps=()):
    n = len(near)
    rows = near[0].shape[0]
    _, inner, width = weight.shape
    slots = rows // peers
    share = inner // n_dp
    tile = wide_tile_of(width)

    def body(*refs):
        near_refs, far_refs = refs[:n], refs[n : 2 * n]
        core_ref, w_ref, hidden, mine, send, *scratch = refs[2 * n :]
        piece = piece_of(w_ref, *scratch, 2)

        @pl.when(pl.program_id(0) == 0)
        def _():
            for at, part_refs in ((0, near_refs), (rows, far_refs)):
                gate_up = total(part_refs)
                gate = gate_up[:, :inner]
                hidden[at : at + rows, :] = (
                    gate * jax.nn.sigmoid(gate) * gate_up[:, inner:]
                ).astype(BF16)
            first = pl.multiple_of(core_ref[0] * share, 128)
            mine[...] = hidden[:, pl.ds(first, share)]

        got = jnp.dot(hidden[...], piece(), preferred_element_type=F32).astype(BF16)
        send[:, :slots, :] = got[rows:].reshape(peers, slots, tile)
        send[:, slots:, :] = got[:rows].reshape(peers, slots, tile)

    return run(
        body,
        (
            jax.ShapeDtypeStruct((2 * rows, inner), BF16),
            jax.ShapeDtypeStruct((2 * rows, share), BF16),
            jax.ShapeDtypeStruct((peers, 2 * slots, width), BF16),
        ),
        (width // tile,),
        [fixed(p.shape) for p in (*near, *far)]
        + [pl.BlockSpec(memory_space=pltpu.SMEM), ANYWHERE],
        (
            fixed((2 * rows, inner)),
            fixed((2 * rows, share)),
            pl.BlockSpec((peers, 2 * slots, tile), lambda c: (0, 0, c)),
        ),
        [*near, *far, core, weight],
        streamed(weight.shape, tile, 2),
        deps=deps,
    )


def place_rows(pieces, place, slots, out, first):
    peers = len(pieces)
    for d, piece in enumerate(pieces):
        for b in range(2):
            at = pl.multiple_of(first + (b * peers + (place ^ d)) * slots, slots)
            out[pl.ds(at, slots), :] = piece[b * slots : (b + 1) * slots, :]


def hidden_grad_part(scalars, near, far, slots, weight, deps=(), flops=0):
    peers = len(near)
    width = near[0].shape[1]
    inner = weight.shape[1]
    rows = 2 * peers * slots
    step = 2 * rows // PARTS
    tile = tile_of(inner)

    def body(scalar_ref, *refs):
        near_refs, far_refs = refs[:peers], refs[peers : 2 * peers]
        w_ref, *outs, x = refs[2 * peers : 2 * peers + PARTS + 2]
        scratch = refs[2 * peers + PARTS + 2 :]
        piece = piece_of(w_ref, *scratch, 1)

        @pl.when(pl.program_id(0) == 0)
        def _():
            place_rows(near_refs, scalar_ref[3], slots, x, 0)
            place_rows(far_refs, scalar_ref[3], slots, x, rows)

        got = lax.dot_general(
            x[...], piece(), (((1,), (1,)), ((), ())), preferred_element_type=F32
        )
        for p, out in enumerate(outs):
            out[...] = got[p * step : (p + 1) * step].astype(BF16)

    return run(
        body,
        [jax.ShapeDtypeStruct((step, inner), BF16)] * PARTS
        + [jax.ShapeDtypeStruct((2 * rows, width), BF16)],
        (inner // tile,),
        [pl.BlockSpec(memory_space=pltpu.SMEM)]
        + [fixed((2 * slots, width))] * (2 * peers)
        + [ANYWHERE],
        [pl.BlockSpec((step, tile), lambda c: (0, c))] * PARTS + [fixed((2 * rows, width))],
        [scalars, *near, *far, weight],
        streamed(weight.shape, tile, 1),
        deps,
        flops=flops,
    )


def rows_dx(grad_parts, near, far, weight, peers, deps=()):
    n = len(near)
    rows = near[0].shape[0]
    inner = grad_parts[0][0].shape[1]
    step = 2 * rows // PARTS
    width = weight.shape[1]
    slots = rows // peers
    tile = tile_of(width)
    blocks = pl.BlockSpec((peers, 2 * slots, tile), lambda c: (0, 0, c))

    def body(*refs):
        grad_refs, refs = refs[: PARTS * n], refs[PARTS * n :]
        near_refs, far_refs = refs[:n], refs[n : 2 * n]
        w_ref, out, both, *scratch = refs[2 * n :]
        piece = piece_of(w_ref, *scratch, 1)

        @pl.when(pl.program_id(0) == 0)
        def _():
            for p in range(PARTS):
                hidden_grad = total(grad_refs[p * n : (p + 1) * n])
                part_refs, at = (near_refs, p * step) if p * step < rows else (far_refs, p * step - rows)
                gate_up = total([ref.at[at : at + step, :] for ref in part_refs])
                gate, up = gate_up[:, :inner], gate_up[:, inner:]
                sig = jax.nn.sigmoid(gate)
                gate_grad = hidden_grad * up * sig * (1.0 + gate * (1.0 - sig))
                both[p * step : (p + 1) * step, :inner] = gate_grad.astype(BF16)
                both[p * step : (p + 1) * step, inner:] = (hidden_grad * (gate * sig)).astype(BF16)

        got = lax.dot_general(
            both[...],
            piece(),
            (((1,), (1,)), ((), ())),
            preferred_element_type=F32,
        ).astype(BF16)
        out[:, :slots, :] = got[rows:].reshape(peers, slots, tile)
        out[:, slots:, :] = got[:rows].reshape(peers, slots, tile)

    return run(
        body,
        jax.ShapeDtypeStruct((peers, 2 * slots, width), BF16),
        (width // tile,),
        [fixed(p.shape) for p in (*sum(grad_parts, []), *near, *far)] + [ANYWHERE],
        blocks,
        [*sum(grad_parts, []), *near, *far, weight],
        [pltpu.VMEM((2 * rows, 2 * inner), BF16)] + streamed(weight.shape, tile, 1),
        deps,
    )


def give(back, group, slots, matrices, more=None, deps=()):
    peers, _, width = back.shape
    count = matrices[0].shape[0]
    tile = wide_tile_of(width)
    column = pl.BlockSpec((count, tile), lambda c: (0, c))

    def body(back_ref, *refs):
        data = back_ref[...].reshape(peers * slots, tile)
        result = jnp.dot(refs[0][...], data, preferred_element_type=F32)
        for ref in refs[1 : len(matrices)]:
            result = result + jnp.dot(ref[...], data, preferred_element_type=F32)
        if more is not None:
            result = result + refs[len(matrices)][...].astype(F32)
        refs[-1][...] = result.astype(BF16)

    return run(
        body,
        jax.ShapeDtypeStruct((count, width), BF16),
        (width // tile,),
        [pl.BlockSpec((peers, slots, tile), lambda c: (0, group, c))]
        + [fixed(m.shape) for m in matrices]
        + ([column] if more is not None else []),
        column,
        [back] + list(matrices) + ([more] if more is not None else []),
        deps=deps,
    )


def finish(back_out, back_dx, slots, weighted, plain, out_from, dx_from, deps=()):
    peers, _, width = back_out.shape
    count = plain.shape[0]
    tile = wide_tile_of(width)
    column = pl.BlockSpec((count, tile), lambda c: (0, c))

    def body(back_ref, back_dx_ref, high, low, plain_ref, out_ref, dx_ref, layer_out, token_grad):
        rows = back_ref[...].reshape(peers * slots, tile)
        result = jnp.dot(high[...], rows, preferred_element_type=F32)
        result = result + jnp.dot(low[...], rows, preferred_element_type=F32)
        layer_out[...] = (result + out_ref[...].astype(F32)).astype(BF16)
        rows = back_dx_ref[...].reshape(peers * slots, tile)
        result = jnp.dot(plain_ref[...], rows, preferred_element_type=F32)
        token_grad[...] = (result + dx_ref[...].astype(F32)).astype(BF16)

    return run(
        body,
        [jax.ShapeDtypeStruct((count, width), BF16)] * 2,
        (width // tile,),
        [pl.BlockSpec((peers, slots, tile), lambda c: (0, 1, c))] * 2
        + [fixed(plain.shape)] * 3
        + [column] * 2,
        [column] * 2,
        [back_out, back_dx, *weighted, plain, out_from, dx_from],
        deps=deps,
    )


def expert_grad(where, hidden, far_shares, own, there, slots, deps=(), flops=0):
    n, peers = len(far_shares), len(there)
    rows, width = own.shape
    share = hidden.shape[1] // n
    tile = wide_tile_of(width)

    def body(where_ref, hidden_ref, *refs):
        share_refs, own_ref = refs[:n], refs[n]
        there_refs = refs[n + 1 : n + 1 + peers]
        out, left, right = refs[-3:]
        moved = where_ref[1] != 0
        at = pl.program_id(1)

        @pl.when(pl.program_id(0) == 0)
        def _():
            @pl.when(jnp.logical_not(moved))
            def _():
                left[at] = hidden_ref[...].astype(F32).T.astype(BF16)

            for d in range(n):
                @pl.when(jnp.logical_and(moved, at == d))
                def _():
                    left[at] = share_refs[d][...].astype(F32).T.astype(BF16)

        @pl.when(jnp.logical_and(moved, at == 0))
        def _():
            place_rows([r.at[2 * slots :, :] for r in there_refs], where_ref[2], slots, right, 0)
            place_rows(there_refs, where_ref[2], slots, right, rows // 2)

        @pl.when(jnp.logical_and(jnp.logical_not(moved), at == 0))
        def _():
            right[...] = own_ref[...]

        out[0] = jnp.dot(left[at], right[...], preferred_element_type=F32).astype(BF16)

    def place(d, where):
        return lax.rem(where[0] - d + n, n)

    return pl.pallas_call(
        body,
        out_shape=pltpu.HBM((1, hidden.shape[1], width), BF16),
        grid_spec=pltpu.PrefetchScalarGridSpec(
            num_scalar_prefetch=1,
            grid=(width // tile, n),
            in_specs=[pl.BlockSpec((rows, share), lambda c, d, w: (0, place(d, w)))]
            + [pl.BlockSpec((rows, share), lambda c, d, w: (0, 0))] * n
            + [pl.BlockSpec((rows, tile), lambda c, d, w: (0, c))]
            + [pl.BlockSpec((4 * slots, tile), lambda c, d, w: (0, c))] * peers
            + [ANYWHERE] * len(deps),
            out_specs=pl.BlockSpec((1, share, tile), lambda c, d, w: (0, place(d, w), c)),
            scratch_shapes=[pltpu.VMEM((n, share, rows), BF16), pltpu.VMEM((rows, tile), BF16)],
        ),
        cost_estimate=pl.CostEstimate(flops=flops, bytes_accessed=0, transcendentals=0),
        compiler_params=pltpu.CompilerParams(vmem_limit_bytes=50 * 1024 * 1024),
    )(where, hidden, *far_shares, own, *there, *deps)


def crossed(block, axis, distance):
    size = lax.axis_size(axis)
    return lax.ppermute(block, axis, [(i, (i + distance) % size) for i in range(size)])


def over_dp(part):
    parts = [part] + [crossed(part, "dp", d) for d in range(1, lax.axis_size("dp"))]
    if len(parts) > 2:
        parts = [sum(p.astype(F32) for p in parts)]
    return parts


def chosen(routes, weights, expert, slots):
    count = routes[0].shape[1]
    earlier = lax.broadcasted_iota(jnp.int32, (count, count), 0)
    later = lax.broadcasted_iota(jnp.int32, (count, count), 1)
    before = (earlier < later).astype(F32).astype(BF16)
    peers = expert.shape[0]
    expert = expert.astype(F32)
    member = jnp.zeros((peers, count), F32)
    table = jnp.zeros((peers, count), F32)
    for route, weight in zip(routes, weights):
        named = route == expert
        member = jnp.where(named, 1.0, member)
        table = jnp.where(named, weight, table)
    place = jnp.dot(member.astype(BF16), before, preferred_element_type=F32)
    place = jnp.where(member > 0.0, place, -1.0)
    slot = lax.broadcasted_iota(jnp.int32, (slots, count), 0).astype(F32)
    hits = [slot == place[e : e + 1, :] for e in range(peers)]
    sel = jnp.concatenate([jnp.where(hit, 1.0, 0.0) for hit in hits], axis=0)
    weighted = [jnp.where(hit, table[e : e + 1, :], 0.0) for e, hit in enumerate(hits)]
    return sel, jnp.concatenate(weighted, axis=0)


def dispatch_tokens(table, first, peers, slots, tokens, deps=(), flops=0):
    count, width = tokens.shape
    top_count = table.shape[0] // 2
    rows = peers * slots

    def body(first_ref, table_ref, tokens_ref, send, plain, high, low):
        names = [table_ref[k : k + 1, :] for k in range(2 * top_count)]
        expert = first_ref[0] + lax.broadcasted_iota(jnp.int32, (peers, count), 0)
        sel, weighted = chosen(names[:top_count], names[top_count:], expert, slots)
        got = jnp.dot(sel.astype(BF16), tokens_ref[...], preferred_element_type=F32)
        send[...] = got.astype(BF16).reshape(peers, slots, width)
        plain[...] = sel.T.astype(BF16)
        turned = weighted.T
        top = turned.astype(BF16)
        high[...] = top
        low[...] = (turned - top.astype(F32)).astype(BF16)

    shapes = [((peers, slots, width), BF16)] + [((count, rows), BF16)] * 3
    return run(
        body,
        [jax.ShapeDtypeStruct(*shape) for shape in shapes],
        (1,),
        [pl.BlockSpec(memory_space=pltpu.SMEM), fixed(table.shape), fixed(tokens.shape)],
        [fixed(shape) for shape, _ in shapes],
        [first, table, tokens],
        deps=deps,
        flops=flops,
    )


def dispatch_grads(scalars, table, table_next, own, beside, peers, slots, into=None, deps=(), flops=0):
    top_count = table.shape[0] // 2
    count, width = own.shape

    def body(scalar_ref, table_ref, next_ref, own_ref, beside_ref, *refs):
        *outs, data, names = refs[len(into or ()) :]
        for swap in (0, 1):

            @pl.when(scalar_ref[2] == swap)
            def _():
                for m in range(2):
                    data[m] = (own_ref, beside_ref)[m ^ swap][...]
                    names[m] = (table_ref, next_ref)[m ^ swap][...]

        place = lax.broadcasted_iota(jnp.int32, (peers, count), 0) ^ scalar_ref[3]
        for b in range(2):
            route = [names[b, k : k + 1, :] for k in range(top_count)]
            weight = [names[b, top_count + k : top_count + k + 1, :] for k in range(top_count)]
            for trade in (0, 1):
                sel, weighted = chosen(route, weight, scalar_ref[trade] + place, slots)
                got = jnp.dot(sel.astype(BF16), data[b], preferred_element_type=F32)
                got = (got * jnp.sum(weighted, axis=1, keepdims=True)).astype(BF16)
                for d in range(peers):
                    out = outs[trade * peers + d]
                    out[b * slots : (b + 1) * slots, :] = got[d * slots : (d + 1) * slots, :]

    operands = [scalars, table, table_next, own, beside]
    specs = [pl.BlockSpec(memory_space=pltpu.SMEM)] + [fixed(x.shape) for x in operands[1:]]
    part = 0 if into is None else 1
    aliases = {len(operands) + d: peers + d for d in range(peers * part)}
    out = run(
        body,
        [jax.ShapeDtypeStruct((2 * slots, width), BF16)] * peers
        + [jax.ShapeDtypeStruct((4 * slots, width), BF16)] * peers,
        (1,),
        specs + [ANYWHERE] * (peers * part),
        [fixed((2 * slots, width))] * peers
        + [pl.BlockSpec((2 * slots, width), lambda c: (part, 0))] * peers,
        operands + list(into or ()),
        [pltpu.VMEM((2, count, width), BF16), pltpu.VMEM((2, 2 * top_count, count), F32)],
        deps,
        aliases,
        flops,
    )
    return out[:peers], out[peers:]


def on_device(tokens, out_grad, gate_up_weight, down_weight, routes, route_weight, swapped):
    experts = lax.axis_size("expert")
    n_dp = lax.axis_size("dp")
    half, plane = experts // 2, experts // 4
    token_count = tokens.shape[0]
    top_count = routes.shape[1]
    slots = max(16, 2 * token_count * top_count // experts)
    me = lax.axis_index("expert").astype(jnp.int32)
    core = lax.axis_index("dp").astype(jnp.int32)
    moved = jnp.any(swapped == me % half).astype(jnp.int32)
    here = (me // half) * half
    layer = (me // plane) * plane
    halves = [[s * half + j for j in range(half)] for s in range(2)]

    def cross(x):
        return crossed(x, "expert", half)

    def beside(x):
        return lax.ppermute(x, "expert", [(i, i ^ plane) for i in range(experts)])

    def exchange(x):
        return lax.all_to_all(
            x, "expert", split_axis=0, concat_axis=0, tiled=True, axis_index_groups=halves
        )

    def over_plane(pieces):
        return [pieces[0]] + [
            lax.ppermute(pieces[d], "expert", [(i, i ^ d) for i in range(experts)])
            for d in range(1, plane)
        ]

    tokens_far = cross(tokens)
    table = jnp.concatenate([routes.T.astype(F32), route_weight.T], axis=0)
    table_far = cross(table)
    table_beside = beside(table)
    table_corner = lax.ppermute(
        table, "expert", [(i, (i ^ plane) ^ half) for i in range(experts)]
    )
    grad_beside = beside(out_grad)
    first_at = here.reshape(1)
    scalars = jnp.stack([layer, (layer + half) % experts, (me // plane) % 2, me % plane])
    where = jnp.stack([core, moved, me % plane])

    send_1, back_sel_n, *back_wt_n = dispatch_tokens(table, first_at, half, slots, tokens)
    first = exchange(send_1)
    send_near, trade_near = dispatch_grads(
        scalars, table, table_beside, out_grad, grad_beside, plane, slots, deps=(send_1, table_corner)
    )
    grads_near = over_plane(send_near)
    grad_copy = held(out_grad, tokens_far, send_near[0])
    grad_far = cross(grad_copy)
    send_2, back_sel_f, *back_wt_f = dispatch_tokens(
        table_far, first_at, half, slots, tokens_far, deps=(grad_copy,), flops=LONG
    )
    send_2 = tied(send_2, first)
    second = exchange(send_2)
    part_n = gate_up_part(first, 0, slots, gate_up_weight, deps=(send_2,))
    parts_n = over_dp(part_n)
    grad_far = tied(grad_far, part_n, flops=LONG)
    far_beside = beside(grad_far)
    part_f = gate_up_part(second, 0, slots, gate_up_weight, deps=(part_n,))
    parts_f = over_dp(part_f)

    send_far, trade = dispatch_grads(
        scalars,
        table_far,
        table_corner,
        grad_far,
        far_beside,
        plane,
        slots,
        into=trade_near,
        deps=(part_f, *grads_near[1:]),
        flops=LONG,
    )
    grads_far = over_plane(send_far)
    hidden, share, send_4 = hidden_and_out(
        parts_n, parts_f, down_weight, core.reshape(1), n_dp, half, deps=(send_far[0],)
    )
    far_share = cross(share)
    send_4 = tied(send_4, second)
    fourth = exchange(send_4)

    *grad_part, grads = hidden_grad_part(
        scalars, grads_near, grads_far, slots, down_weight, deps=(send_4,), flops=LONG
    )
    grad_parts = [over_dp(part) for part in grad_part]
    send_5 = rows_dx(grad_parts, parts_n, parts_f, gate_up_weight, half)
    send_5 = tied(send_5, fourth, far_share)
    fifth = exchange(send_5)
    far_shares = [far_share] + [crossed(far_share, "dp", d) for d in range(1, n_dp)]
    give_out = give(fourth, 0, slots, back_wt_f, deps=(send_5,))
    out_from = cross(give_out)

    give_dx = give(fifth, 0, slots, [back_sel_f], deps=(out_from,))
    dx_from = cross(give_dx)
    down_grad = expert_grad(
        where, hidden, far_shares, grads, over_plane(trade), slots, deps=(give_dx,)
    )
    layer_out, token_grad = finish(
        fourth, fifth, slots, back_wt_n, back_sel_n, out_from, dx_from, deps=(down_grad,)
    )
    return layer_out, token_grad, down_grad


def solution(mesh):
    return jax.shard_map(
        on_device,
        mesh=mesh,
        in_specs=(
            P("expert", "dp"),
            P("expert", "dp"),
            P("expert", "dp", None),
            P("expert", None, "dp"),
            P("expert", None),
            P("expert", None),
            P(),
        ),
        out_specs=(P("expert", "dp"), P("expert", "dp"), P("expert", None, "dp")),
        check_vma=False,
    )
```
